32 devices in a mesh: img: 8 (over z, y), cls: 4 (over x, core).
Axes of the slice: x: 2, y: 2, z: 4, core: 2. Of those that a mesh axis runs over, the one named last changes fastest.
Arguments:
- embeddings: bfloat16 [768, 1024], P('img'), may hold values from -128 to 128
- class_text_embedding: bfloat16 [1024, 21888], P(None, 'cls'), may hold values from -1 to 1
- neighbours: int32 [768, 10], P('img'), may hold values from 0 to 223, as said below
- weights: float32 [768, 10], P('img'), may hold values from 0.2 to 1
- requests: int32 [8, 8, 16], P('img'), may hold values from -1 to 95, as said below
Outputs:
- labels: float32 [768, 21888], P('img', 'cls')
The draws below stay inside these ranges and needn't reach their ends.
Inputs may be any that keep to these rules, and one draw needn't show every extreme that they name: requests[d, p, j] is a row index within device p's 96 rows, or -1 for an empty slot; the live slots of each (d, p) come first; requests[d, d] is empty; every d fills all 16 slots for one p. `neighbours`: a slot of 96 or more names a live request slot of the row's own device.
All inputs are finite; a program needn't handle non-finite values.
Results may differ from the reference program's by a relative error of at most 0.00085.
Values may be sent and summed in bfloat16 or wider, within the bound.
No kernel may reach another device: no remote copies, remote signals or barrier semaphores. Data moves between devices by JAX's collectives and lax.ppermute only.
A program may use at most 128 MiB of HBM per device.

```python
import math
import jax
import jax.numpy as jnp
from jax import lax

D = 1024
CLASS_COLUMNS = 21888
LIVE = 21841
ROW_DEV = 96
K = 10
CAP = 16
PEERS = 8
IMAGE_ROWS = 768


def draw_embeddings(key, part):
    key_offset, key_scale = jax.random.split(jax.random.fold_in(key, 5))
    scale_factor = jnp.exp(jax.random.uniform(key_scale, (IMAGE_ROWS, 1), jnp.float32, math.log(0.15), math.log(1.5)))
    values = jnp.clip(jax.random.normal(key_offset, (IMAGE_ROWS, D), jnp.float32) * 3.0, -18.0, 18.0) * scale_factor
    return values.astype(jnp.bfloat16)


def draw_class_text_embedding(key, part):
    key_offset = jax.random.fold_in(jax.random.fold_in(key, 9), 0)
    values = jnp.clip(jax.random.normal(key_offset, (D, CLASS_COLUMNS), jnp.float32), -6.0, 6.0) / math.sqrt(D)
    return values.astype(jnp.bfloat16)


def graph_tables(key):
    keys = jax.random.split(jax.random.fold_in(key, 11), 9)
    counts = jax.random.randint(keys[0], (PEERS, PEERS), 0, CAP + 1)
    full_src = (jnp.arange(PEERS) + 1 + jax.random.randint(keys[1], (PEERS,), 0, PEERS - 1)) % PEERS
    chosen = jax.random.randint(keys[6], (), 0, PEERS - 1)
    full_src = jnp.where(jnp.arange(PEERS) == chosen, PEERS - 1, full_src)
    src_ids = jnp.arange(PEERS)
    counts = jnp.where(src_ids[None, :] == full_src[:, None], CAP, counts)
    counts = jnp.where(src_ids[None, :] == src_ids[:, None], 0, counts)
    slot = jnp.arange(CAP)
    asked = jax.random.randint(keys[2], (PEERS, PEERS, CAP), 0, ROW_DEV)
    requests = jnp.where(slot[None, None, :] < counts[:, :, None], asked, -1).astype(jnp.int32)
    livecount = jnp.sum(counts, axis=1)
    ending = jnp.cumsum(counts, axis=1)
    starting = ending - counts
    device = jnp.arange(IMAGE_ROWS) // ROW_DEV
    pick = jax.random.randint(keys[3], (IMAGE_ROWS, K), 0, 1 << 20) % livecount[device][:, None]
    source = jnp.sum(ending[device][:, None, :] <= pick[:, :, None], axis=-1)
    begin = jnp.take_along_axis(starting[device], source, axis=1)
    remote_slot = ROW_DEV + source * CAP + (pick - begin)
    local_slot = jax.random.randint(keys[4], (IMAGE_ROWS, K), 0, ROW_DEV)
    is_local = jax.random.randint(keys[5], (IMAGE_ROWS, K), 0, 2) == 0
    neighbours = jnp.where(is_local, local_slot, remote_slot)
    forced_row = chosen * ROW_DEV + jax.random.randint(keys[7], (), 0, ROW_DEV)
    forced_col = jax.random.randint(keys[8], (), 0, K)
    row_hit = (jnp.arange(IMAGE_ROWS) == forced_row)[:, None]
    column_ids = jnp.arange(K)[None, :]
    neighbours = jnp.where(row_hit & (column_ids == forced_col), ROW_DEV + PEERS * CAP - 1, neighbours)
    neighbours = jnp.where(row_hit & (column_ids == (forced_col + 1) % K), 0, neighbours)
    return (neighbours.astype(jnp.int32), requests)


def draw_neighbours(key, part):
    return graph_tables(key)[0]


def draw_requests(key, part):
    return graph_tables(key)[1]


def levels(rng, dims, cuts, low, high):
    loudness = 1.0
    for position, shards_of in cuts:
        steps = jax.random.uniform(jax.random.fold_in(jax.random.fold_in(rng, 6), position), (shards_of,), jnp.float32, low / len(cuts), high / len(cuts))
        loudness = loudness * jnp.repeat(jnp.exp(steps), dims[position] // shards_of).reshape((-1,) + (1,) * (len(dims) - 1 - position))
    return loudness


def setup_inputs(seed: int = 0) -> dict:
    key_list = jax.random.split(jax.random.key(seed), 6)
    return {
        "embeddings": draw_embeddings(jax.random.fold_in(key_list[5], 71), 0),
        "class_text_embedding": draw_class_text_embedding(jax.random.fold_in(key_list[5], 71), 0),
        "neighbours": draw_neighbours(jax.random.fold_in(key_list[5], 71), 0),
        "weights": jnp.clip(jnp.exp(math.log(1.0) - 1.609438 * jax.random.uniform(key_list[3], (IMAGE_ROWS, K), jnp.float32) ** levels(key_list[3], (IMAGE_ROWS, K), ((0, 8),), -0.2, 0.2)), 0.2, 1.0),
        "requests": draw_requests(jax.random.fold_in(key_list[5], 71), 0),
    }


smoothing = 1.0


def probabilities(block, class_text_embedding):
    logits = jnp.dot(block, class_text_embedding, preferred_element_type=jnp.float32)
    live = (jnp.arange(CLASS_COLUMNS) < LIVE)[None, :]
    masked = jnp.where(live, logits, -1e30)
    top = jnp.max(masked, axis=1, keepdims=True)
    powers = jnp.where(live, jnp.exp(masked - top), 0.0)
    total = jnp.sum(powers, axis=1, keepdims=True)
    return powers / total


def reference(embeddings, class_text_embedding, neighbours, weights, requests):
    blocks = embeddings.reshape(PEERS, ROW_DEV, D)
    first = lax.map(lambda b: probabilities(b, class_text_embedding), blocks).reshape(IMAGE_ROWS, CLASS_COLUMNS)
    device = (jnp.arange(IMAGE_ROWS) // ROW_DEV).astype(jnp.int32)[:, None]
    offset = neighbours - ROW_DEV
    remote = offset >= 0
    clipped = jnp.maximum(offset, 0)
    source = (clipped // CAP).astype(jnp.int32)
    within = (clipped % CAP).astype(jnp.int32)
    asked = requests[device, source, within]
    glob = jnp.where(remote, source * ROW_DEV + asked, device * ROW_DEV + neighbours).astype(jnp.int32)

    def sweep(previous):
        def one(items):
            index, edge, own = items
            acc = jnp.zeros((ROW_DEV, CLASS_COLUMNS), jnp.float32)
            for k in range(K):
                acc = acc + edge[:, k:k + 1] * previous[index[:, k]]
            degree = jnp.sum(edge, axis=1, keepdims=True)
            return (own + smoothing * acc) / (1.0 + smoothing * degree)

        return lax.map(one, (glob.reshape(PEERS, ROW_DEV, K), weights.reshape(PEERS, ROW_DEV, K),
                             first.reshape(PEERS, ROW_DEV, CLASS_COLUMNS))).reshape(IMAGE_ROWS, CLASS_COLUMNS)

    second = sweep(first)
    return sweep(second)
```

```python
import functools
import jax
import jax.numpy as jnp
from jax import lax
from jax.experimental import pallas as pl
from jax.experimental.pallas import tpu as pltpu
from jax.sharding import PartitionSpec as P

LIVE = 21841
SMOOTHING = 1.0
TILE = 512
LANES = 128
CHUNK = 128
NT = (((1,), (1,)), ((), ()))
GROUP = 32
f32, bf16 = jnp.float32, jnp.bfloat16
VMEM = pltpu.VMEM
WHOLE = pl.BlockSpec(memory_space=VMEM)
SCALARS = pl.BlockSpec(memory_space=pltpu.SMEM)
ANYWHERE = pl.BlockSpec(memory_space=pl.ANY)
MIB = 2**20


def column_tiles(width):
    return [(a, min(a + TILE, width)) for a in range(0, width, TILE)]


def round_up(n, m):
    return -(-n // m) * m


def resident(x):
    return pltpu.with_memory_space_constraint(x, VMEM)


def exchange_plan(peers):
    bits = peers.bit_length() - 1
    main, newest, stages = [0], [0], []
    for bit in reversed(range(1, bits)):
        step = 1 << bit
        stages.append([(step, list(main)), (1, list(newest))])
        newest = [b ^ step for b in main]
        main = main + newest
    if bits:
        stages.append([(1, list(newest))])
    order = [0] + [b ^ step for stage in stages for step, blocks in stage for b in blocks]
    return stages, order


def table_kernel(here_ref, requests_hbm, e_hbm, neighbours_hbm, weights_hbm, own_ref, mine_ref, table_ref, near_ref, weight_ref, requests_ref, sems):
    core, me = here_ref[1], here_ref[2]
    rows, depth = e_hbm.shape
    peers, cap = requests_hbm.shape
    k = near_ref.shape[0]
    slots = round_up(k, 8)
    moves = (
        (requests_hbm, requests_ref),
        (neighbours_hbm, near_ref),
        (weights_hbm, weight_ref),
        (e_hbm, own_ref.at[:, :depth]),
    )
    copies = [pltpu.make_async_copy(src, dst, sems.at[i]) for i, (src, dst) in enumerate(moves)]
    for copy in copies:
        copy.start()
    table_ref[...] = jnp.zeros_like(table_ref)
    for copy in copies[:3]:
        copy.wait()
    near = near_ref[...]
    slot = near - rows
    block = jnp.zeros_like(near) + me
    within = near
    for p in range(peers):
        block = jnp.where(slot >= p * cap, p, block)
        for j in range(cap):
            within = jnp.where(slot == p * cap + j, requests_ref[p, j], within)
    weight = weight_ref[...]
    w0 = weight.astype(bf16).astype(f32)
    w1 = (weight - w0).astype(bf16).astype(f32)
    w2 = weight - w0 - w1
    for i, x in enumerate((block.astype(f32), within.astype(f32), w0, w1, w2)):
        table_ref[i * slots : i * slots + k, :] = x
    own_ref[:, depth:] = table_ref[...].T.astype(bf16)
    copies[3].wait()
    half = rows // 2
    mine_ref[...] = own_ref[pl.ds(pl.multiple_of(core * half, 16), half), :]


def outside(x):
    return pltpu.with_memory_space_constraint(x, pltpu.HBM)


def with_tables(here, requests, embeddings, neighbours, weights):
    rows, depth = embeddings.shape
    k = neighbours.shape[1]
    return pl.pallas_call(
        table_kernel,
        in_specs=[SCALARS] + [pl.BlockSpec(memory_space=pltpu.HBM)] * 4,
        out_specs=[WHOLE] * 2,
        out_shape=[VMEM((rows, depth + LANES), bf16), VMEM((rows // 2, depth + LANES), bf16)],
        scratch_shapes=[
            VMEM((LANES, rows), f32),
            VMEM((k, rows), jnp.int32),
            VMEM((k, rows), f32),
            pltpu.SMEM(requests.shape, jnp.int32),
            pltpu.SemaphoreType.DMA((4,)),
        ],
        compiler_params=pltpu.CompilerParams(vmem_limit_bytes=MIB),
        name="tables",
    )(here, outside(requests), outside(embeddings), outside(neighbours.T), outside(weights.T))


def powers_kernel(tiles, min_live, depth, first_row, n_parts, first, here_ref, *refs):
    parts, c_ref = refs[:n_parts], refs[n_parts]
    if first:
        hi_ref, lo_ref, tab_ref, top_ref, sum_ref, tile_ref, ct_ref, e_ref, sems = refs[-9:]
        loads = [pltpu.make_async_copy(c_ref.at[a:b, :], ct_ref.at[a:b, :], sems.at[t]) for t, (a, b) in enumerate(tiles)]
        for load in loads:
            load.start()
    else:
        hi_ref, lo_ref, tab_ref, top_ref, sum_ref, tile_ref, e_ref = refs[-7:]
        ct_ref = c_ref
    core = here_ref[1]
    row = 0
    half = parts[-1].shape[0]
    swappable = 0
    for part in parts:
        n = part.shape[0]
        at = row
        if n == half:
            at = pl.multiple_of(row + n * (core if swappable % 2 == 0 else -core), 16)
            swappable += 1
        e_ref[pl.ds(at, n), :] = part[:, :depth]
        tab_ref[pl.ds(first_row + at, n), :] = part[:, depth:].astype(f32)
        row += n
    rows = slice(first_row, first_row + row)
    lane = lax.broadcasted_iota(jnp.int32, (row, LANES), 1)
    tops = jnp.full((row, LANES), -1e30, f32)
    sums = jnp.zeros((row, LANES), f32)
    for t, (a, b) in enumerate(tiles):
        if first:
            loads[t].wait()
        logits = lax.dot_general(e_ref[...], ct_ref[a:b, :], NT, preferred_element_type=f32)
        if b > min_live:
            live = lax.broadcasted_iota(jnp.int32, logits.shape, 1) + a < here_ref[0]
            logits = jnp.where(live, logits, -1e30)
        top = jnp.max(logits, axis=1, keepdims=True)
        powers = jnp.exp(logits - top)
        if b > min_live:
            powers = jnp.where(live, powers, 0.0)
        total = jnp.sum(powers, axis=1, keepdims=True)
        hi = powers.astype(bf16)
        hi_ref[rows, a:b] = hi
        lo_ref[rows, a:b] = (powers - hi.astype(f32)).astype(bf16)
        tops = jnp.where(lane == t, top, tops)
        sums = jnp.where(lane == t, total, sums)
    slots = tile_ref.shape[0]
    tops, sums = tops.T[:slots], sums.T[:slots]
    top = jnp.max(tops, axis=0, keepdims=True)
    tile_ref[...] = tops
    top_ref[...] = top
    sum_ref[...] = jnp.sum(sums * jnp.exp(tops - top), axis=0, keepdims=True)


def powers_of(parts, classes, here, buffers, first_row, total_rows, min_live):
    first = buffers is None
    width, depth = classes.shape
    rows = sum(p.shape[0] for p in parts)
    tiles = column_tiles(width)
    slots = round_up(len(tiles), 8)
    n = len(parts)
    aliased = [] if first else list(buffers)
    out_shape = [
        VMEM((total_rows, width), bf16),
        VMEM((total_rows, width), bf16),
        VMEM((total_rows, LANES), f32),
        VMEM((1, rows), f32),
        VMEM((1, rows), f32),
        VMEM((slots, rows), f32),
    ]
    scratch = [VMEM((rows, depth), bf16)]
    limit = 4 * MIB
    if first:
        out_shape.append(VMEM((width, depth), bf16))
        scratch.append(pltpu.SemaphoreType.DMA((len(tiles),)))
    return pl.pallas_call(
        functools.partial(powers_kernel, tiles, min_live, depth, first_row, n, first),
        in_specs=[SCALARS] + [WHOLE] * n + [pl.BlockSpec(memory_space=pltpu.HBM) if first else WHOLE] + [WHOLE] * len(aliased),
        out_specs=[WHOLE] * len(out_shape),
        out_shape=out_shape,
        scratch_shapes=scratch,
        input_output_aliases={2 + n + i: i for i in range(len(aliased))},
        compiler_params=pltpu.CompilerParams(vmem_limit_bytes=limit),
        cost_estimate=pl.CostEstimate(flops=2 * rows * width * depth, bytes_accessed=rows * depth * 2, transcendentals=rows * width),
        name="powers",
    )(here, *[resident(p) for p in parts], outside(classes) if first else resident(classes), *[resident(b) for b in aliased])


def split(x):
    hi = x.astype(bf16)
    return hi, (x - hi.astype(f32)).astype(bf16)


def dot(a, b):
    return jnp.dot(a, b, preferred_element_type=f32)


def graph_kernel(order, here_ref, requests_ref, tab_ref, near_ref, weight_ref, m_ref, w_ref, asked_ref, rows_ref):
    me = here_ref[2]
    peers, cap = requests_ref.shape
    total_rows = tab_ref.shape[0]
    k, rows_here = near_ref.shape
    slots = round_up(k, 8)
    extended = rows_here + peers * cap

    def place_of(block, within):
        relative = block ^ me
        place = jnp.zeros_like(block)
        for i, b in enumerate(order):
            place = jnp.where(relative == b, i * rows_here, place)
        return place + within

    asked_ref[...] = jnp.full_like(asked_ref, -1)
    lane = lax.broadcasted_iota(jnp.int32, (1, LANES), 1)
    for p in range(peers):
        start = place_of(jnp.full((1, 1), p, jnp.int32), 0)
        row = jnp.full((1, LANES), -1, jnp.int32)
        for j in range(cap):
            row = jnp.where(lane == j, requests_ref[p, j], row)
        asked_ref[p : p + 1, :] = jnp.where(row >= 0, row + start, -1)
    asked = asked_ref[...].T
    column = lax.broadcasted_iota(jnp.int32, (cap, total_rows), 1)
    tab = tab_ref[...].astype(bf16)
    rows_ref[:rows_here, :] = tab_ref[:rows_here, :]
    picks = [jnp.where(column == asked[:cap, p : p + 1], 1.0, 0.0).astype(bf16) for p in range(peers)]
    rows_ref[rows_here:, :] = dot(jnp.concatenate(picks, axis=0), tab)

    near, weight = near_ref[...].T, weight_ref[...].T
    column = lax.broadcasted_iota(jnp.int32, (rows_here, extended), 1)
    acc = jnp.zeros((rows_here, extended), f32)
    for i in range(k):
        acc = acc + jnp.where(column == near[:, i : i + 1], SMOOTHING * weight[:, i : i + 1], 0.0)
    degree = jnp.sum(weight, axis=1, keepdims=True)
    scale = 1.0 / (1.0 + SMOOTHING * degree)
    w_ref[...] = acc * scale
    column = lax.broadcasted_iota(jnp.int32, (rows_here, total_rows), 1)
    sub = lax.broadcasted_iota(jnp.int32, (rows_here, total_rows), 0)
    m_ref[...] = jnp.where(column == sub, scale, 0.0)

    for start in range(0, extended, GROUP):
        tab = rows_ref[start : start + GROUP, :]
        within = pltpu.roll(tab, LANES - slots, 1).astype(jnp.int32)
        weight = pltpu.roll(tab, LANES - 2 * slots, 1) + pltpu.roll(tab, LANES - 3 * slots, 1) + pltpu.roll(tab, LANES - 4 * slots, 1)
        place = place_of(tab.astype(jnp.int32), within)
        column = lax.broadcasted_iota(jnp.int32, (GROUP, total_rows), 1)
        if start < rows_here:
            itself = lax.broadcasted_iota(jnp.int32, (GROUP, 1), 0) + start
        else:
            itself = jnp.concatenate([asked[:cap, p : p + 1] for p in range((start - rows_here) // cap, (start - rows_here + GROUP) // cap)], axis=0)
        acc = jnp.where(column == itself, 1.0, 0.0)
        degree = jnp.zeros((GROUP, 1), f32)
        for i in range(k):
            w = weight[:, i : i + 1]
            acc = acc + jnp.where(column == place[:, i : i + 1], SMOOTHING * w, 0.0)
            degree = degree + w
        thi, tlo = split(acc / (1.0 + SMOOTHING * degree))
        ahi, alo = split(w_ref[:, start : start + GROUP])
        m_ref[...] += dot(ahi, thi) + dot(alo, thi) + dot(ahi, tlo)


def graph_of(here, requests, tab, neighbours, weights, order):
    total_rows = tab.shape[0]
    rows_here, k = neighbours.shape
    extended = rows_here + requests.size
    return pl.pallas_call(
        functools.partial(graph_kernel, order),
        in_specs=[SCALARS, SCALARS, WHOLE, WHOLE, WHOLE],
        out_specs=WHOLE,
        out_shape=VMEM((rows_here, total_rows), f32),
        scratch_shapes=[VMEM((rows_here, extended), f32), VMEM((LANES, LANES), jnp.int32), VMEM((extended, LANES), f32)],
        compiler_params=pltpu.CompilerParams(vmem_limit_bytes=(4 if total_rows <= 768 else 16) * MIB),
        cost_estimate=pl.CostEstimate(flops=2 * 10**9, bytes_accessed=0, transcendentals=0),
        name="graph",
    )(here, requests, resident(tab), neighbours.T, weights.T)


def apply_kernel(tiles, n_pieces, n_cls, m_ref, hi_ref, lo_ref, *refs):
    tile_refs, top_refs, sum_refs = refs[:n_pieces], refs[n_pieces : 2 * n_pieces], refs[2 * n_pieces : 3 * n_pieces]
    far_refs = refs[3 * n_pieces : 3 * n_pieces + n_cls - 1]
    out_ref, _, _, staged, sems = refs[3 * n_pieces + n_cls - 1 :]
    rows_here = m_ref.shape[0]

    def row(pieces):
        return jnp.concatenate([p[...] for p in pieces], axis=1)

    tops = [row(top_refs)] + [r[0:1, :] for r in far_refs]
    sums = [row(sum_refs)] + [r[1:2, :] for r in far_refs]
    top = functools.reduce(jnp.maximum, tops)
    total = sum(s * jnp.exp(t - top) for s, t in zip(sums, tops))
    factors = jnp.exp(row(tile_refs) - top) / total
    copies = []
    for t, (a, b) in enumerate(tiles):
        whi, wlo = split(m_ref[...] * factors[t : t + 1, :])
        x = dot(jnp.concatenate([whi, wlo], axis=0), hi_ref[:, a:b])
        staged[:, a:b] = x[:rows_here] + x[rows_here:] + dot(whi, lo_ref[:, a:b])
        copy = pltpu.make_async_copy(staged.at[:, a:b], out_ref.at[:, a:b], sems.at[t])
        copy.start()
        copies.append(copy)
    for copy in copies:
        copy.wait()


def applied(m, hi, lo, tile_tops, tops, sums, far):
    rows_here, total_rows = m.shape
    width = hi.shape[1]
    tiles = column_tiles(width)
    operands = [m, hi, lo, *tile_tops, *tops, *sums, *far]
    return pl.pallas_call(
        functools.partial(apply_kernel, tiles, len(tops), len(far) + 1),
        in_specs=[WHOLE] * len(operands),
        out_specs=[ANYWHERE, WHOLE, WHOLE],
        out_shape=[jax.ShapeDtypeStruct((rows_here, width), f32), VMEM(hi.shape, bf16), VMEM(lo.shape, bf16)],
        input_output_aliases={1: 1, 2: 2},
        scratch_shapes=[VMEM((rows_here, width), f32), pltpu.SemaphoreType.DMA((len(tiles),))],
        compiler_params=pltpu.CompilerParams(vmem_limit_bytes=(4 if total_rows <= 768 else 12) * MIB),
        cost_estimate=pl.CostEstimate(flops=6 * rows_here * total_rows * width, bytes_accessed=rows_here * width * 4, transcendentals=0),
        name="smooth",
    )(*[resident(x) for x in operands])[0]


def shards(n_img, n_cls, embeddings, class_text_embedding, neighbours, weights, requests):
    rows_here = embeddings.shape[0]
    width = class_text_embedding.shape[1]
    half = rows_here // 2
    me, col = lax.axis_index("img"), lax.axis_index("cls")
    total_rows = n_img * rows_here
    here = jnp.stack([jnp.minimum(LIVE - col * width, width), col & 1, me]).astype(jnp.int32)
    min_live = min(width, LIVE - (n_cls - 1) * width)

    own, mine = with_tables(here, requests[0], embeddings, neighbours, weights)
    stages, order = exchange_plan(n_img)
    held, pieces = {0: mine}, [[own]]
    for stage in stages:
        sends = []
        for step, blocks in stage:
            sent = held[blocks[0]] if len(blocks) == 1 else jnp.concatenate([held[b] for b in blocks], axis=0)
            sends.append(lax.ppermute(sent, "img", [(i, i ^ step) for i in range(n_img)]))
        sends = lax.optimization_barrier(sends)
        piece = []
        for (step, blocks), got in zip(stage, sends):
            swapped = lax.ppermute(got, "cls", [(i, i ^ 1) for i in range(n_cls)])
            for i, b in enumerate(blocks):
                cut = slice(i * half, (i + 1) * half)
                held[b ^ step] = got[cut]
                piece += [got[cut], swapped[cut]]
        pieces += [piece[i : i + 6] for i in range(0, len(piece), 6)]
    pieces[:2] = [pieces[0] + pieces[1]]

    classes, buffers, first_row, tops, sums, tile_tops = class_text_embedding.T, None, 0, [], [], []
    for i, piece in enumerate(pieces):
        results = powers_of(piece, classes, here, buffers, first_row, total_rows, min_live)
        buffers = results[:3]
        if i == 0:
            classes = results[6]
        first_row += sum(p.shape[0] for p in piece)
        tops.append(results[3])
        sums.append(results[4])
        tile_tops.append(results[5])
    hi, lo, tab = buffers
    stats = jnp.concatenate([jnp.concatenate(tops, axis=1), jnp.concatenate(sums, axis=1)], axis=0)
    far = [lax.ppermute(stats, "cls", [(i, i ^ d) for i in range(n_cls)]) for d in range(1, n_cls)]
    m = graph_of(here, requests[0], tab, neighbours, weights, order)
    return applied(m, hi, lo, tile_tops, tops, sums, far)


def solution(mesh):
    in_specs = (
        P("img", None),
        P(None, "cls"),
        P("img", None),
        P("img", None),
        P("img", None, None),
    )
    sizes = mesh.shape
    run = functools.partial(shards, sizes["img"], sizes["cls"])
    return jax.shard_map(run, mesh=mesh, in_specs=in_specs, out_specs=P("img", "cls"), check_vma=False)
```

```python
import functools
import jax
import jax.numpy as jnp
from jax import lax
from jax.experimental import pallas as pl
from jax.experimental.pallas import tpu as pltpu
from jax.sharding import PartitionSpec as P

LIVE = 21841
SMOOTHING = 1.0
TILE = 512
LANES = 128
CHUNK = 128
DEEP = 3
NT = (((1,), (1,)), ((), ()))
GROUP = 32
f32, bf16 = jnp.float32, jnp.bfloat16
VMEM = pltpu.VMEM
WHOLE = pl.BlockSpec(memory_space=VMEM)
SCALARS = pl.BlockSpec(memory_space=pltpu.SMEM)
ANYWHERE = pl.BlockSpec(memory_space=pl.ANY)
MIB = 2**20
FREE = pl.CostEstimate(flops=1000, bytes_accessed=1000, transcendentals=0)


def column_tiles(width):
    return [(a, min(a + TILE, width)) for a in range(0, width, TILE)]


def round_up(n, m):
    return -(-n // m) * m


def resident(x):
    return pltpu.with_memory_space_constraint(x, VMEM)


def exchange_plan(peers):
    direct = list(range(2, peers, 2))

    def cut(blocks):
        return [blocks[i : i + 4] for i in range(0, len(blocks), 4)]

    return direct + [1, 3], direct[1:], [[0]], cut(direct + [1]), cut([3] + [b ^ 1 for b in direct[1:]])


def streamed_from(width):
    tiles = column_tiles(width)
    return tiles[len(tiles) // 2][0]


def outside(x):
    return pltpu.with_memory_space_constraint(x, pltpu.HBM)


HBM = pl.BlockSpec(memory_space=pltpu.HBM)


def table_kernel(here_ref, requests_hbm, e_hbm, neighbours_hbm, weights_hbm, mine_ref, out_ref, table_ref, near_ref, weight_ref, requests_ref, sems):
    core, me = here_ref[1], here_ref[2]
    rows, depth = e_hbm.shape
    half = rows // 2
    peers, cap = requests_hbm.shape
    k = near_ref.shape[0]
    slots = round_up(k, 8)
    start = pl.multiple_of(core * half, 16)
    moves = (
        (requests_hbm, requests_ref),
        (neighbours_hbm, near_ref),
        (weights_hbm, weight_ref),
        (e_hbm.at[pl.ds(start, half), :], mine_ref.at[:, :depth]),
    )
    copies = [pltpu.make_async_copy(src, dst, sems.at[i]) for i, (src, dst) in enumerate(moves)]
    for copy in copies:
        copy.start()
    table_ref[...] = jnp.zeros_like(table_ref)
    for copy in copies[:3]:
        copy.wait()
    near = near_ref[...]
    slot = near - rows
    block = jnp.zeros_like(near) + me
    within = near
    for p in range(peers):
        block = jnp.where(slot >= p * cap, p, block)
        for j in range(cap):
            within = jnp.where(slot == p * cap + j, requests_ref[p, j], within)
    weight = weight_ref[...]
    w0 = weight.astype(bf16).astype(f32)
    w1 = (weight - w0).astype(bf16).astype(f32)
    w2 = weight - w0 - w1
    for i, x in enumerate((block.astype(f32), within.astype(f32), w0, w1, w2)):
        table_ref[i * slots : i * slots + k, :] = x
    out_ref[...] = table_ref[...].T.astype(bf16)
    mine_ref[:, depth:] = out_ref[pl.ds(start, half), :]
    copies[3].wait()


def tables_of(here, requests, embeddings, neighbours, weights):
    rows, depth = embeddings.shape
    k = neighbours.shape[1]
    return pl.pallas_call(
        table_kernel,
        in_specs=[SCALARS] + [HBM] * 4,
        out_specs=[WHOLE] * 2,
        out_shape=[VMEM((rows // 2, depth + LANES), bf16), VMEM((rows, LANES), bf16)],
        scratch_shapes=[
            VMEM((LANES, rows), f32),
            VMEM((k, rows), jnp.int32),
            VMEM((k, rows), f32),
            pltpu.SMEM(requests.shape, jnp.int32),
            pltpu.SemaphoreType.DMA((4,)),
        ],
        compiler_params=pltpu.CompilerParams(vmem_limit_bytes=MIB),
        cost_estimate=FREE,
        name="tables",
    )(here, outside(requests), outside(embeddings), outside(neighbours.T), outside(weights.T))


def split(x):
    hi = x.astype(bf16)
    return hi, (x - hi.astype(f32)).astype(bf16)


def dot(a, b):
    return jnp.dot(a, b, preferred_element_type=f32)


def powers_kernel(tiles, min_live, depth, first_row, n_parts, first, here_ref, *refs):
    parts, ct_ref = refs[:n_parts], refs[n_parts]
    if first:
        c_ref = refs[n_parts + 1]
        p_ref, tab_ref, top_ref, sum_ref, tile_ref, ct_ref, e_ref, sem = refs[-8:]
        split_at = streamed_from(c_ref.shape[0])
        load = pltpu.make_async_copy(c_ref.at[split_at:, :], ct_ref.at[split_at:, :], sem)
        load.start()
    else:
        p_ref, tab_ref, top_ref, sum_ref, tile_ref, e_ref = refs[-6:]
    core = here_ref[1]
    row = 0
    for i, part in enumerate(parts):
        n, at = part.shape[0], row
        if not first or i > 0:
            at = pl.multiple_of(row + n * (core if i % 2 == first else -core), 16)
        e_ref[pl.ds(at, n), :] = part[:, :depth]
        tab_ref[pl.ds(first_row + at, n), :] = part[:, depth:].astype(f32)
        row += n
    rows = slice(first_row, first_row + row)
    lane = lax.broadcasted_iota(jnp.int32, (row, LANES), 1)
    tops = jnp.full((row, LANES), -1e30, f32)
    sums = jnp.zeros((row, LANES), f32)
    for t, (a, b) in enumerate(tiles):
        if first and a == split_at:
            load.wait()
        logits = lax.dot_general(e_ref[...], ct_ref[a:b, :], NT, preferred_element_type=f32)
        if b > min_live:
            live = lax.broadcasted_iota(jnp.int32, logits.shape, 1) + a < here_ref[0]
            logits = jnp.where(live, logits, -1e30)
        top = jnp.max(logits, axis=1, keepdims=True)
        powers = jnp.exp(logits - top)
        if b > min_live:
            powers = jnp.where(live, powers, 0.0)
        p_ref[rows, a:b] = powers
        tops = jnp.where(lane == t, top, tops)
        sums = jnp.where(lane == t, jnp.sum(powers, axis=1, keepdims=True), sums)
    slots = tile_ref.shape[0]
    tops, sums = tops.T[:slots], sums.T[:slots]
    top = jnp.max(tops, axis=0, keepdims=True)
    tile_ref[...] = tops
    top_ref[...] = top
    sum_ref[...] = jnp.sum(sums * jnp.exp(tops - top), axis=0, keepdims=True)


def powers_of(parts, ct, classes, here, buffers, first_row, total_rows, min_live):
    first = buffers is None
    width, depth = ct.shape
    rows = sum(p.shape[0] for p in parts)
    tiles = column_tiles(width)
    slots = round_up(len(tiles), 8)
    n = len(parts)
    aliased = [] if first else list(buffers)
    out_shape = [
        VMEM((total_rows, width), f32),
        VMEM((total_rows, LANES), f32),
        VMEM((1, rows), f32),
        VMEM((1, rows), f32),
        VMEM((slots, rows), f32),
    ]
    scratch = [VMEM((rows, depth), bf16)]
    aliases = {2 + n + i: i for i in range(len(aliased))}
    if first:
        out_shape.append(VMEM((width, depth), bf16))
        scratch.append(pltpu.SemaphoreType.DMA)
        aliases = {1 + n: 5}
    return pl.pallas_call(
        functools.partial(powers_kernel, tiles, min_live, depth, first_row, n, first),
        in_specs=[SCALARS] + [WHOLE] * (n + 1) + ([HBM] if first else [WHOLE] * len(aliased)),
        out_specs=[WHOLE] * len(out_shape),
        out_shape=out_shape,
        scratch_shapes=scratch,
        input_output_aliases=aliases,
        compiler_params=pltpu.CompilerParams(vmem_limit_bytes=8 * MIB),
        cost_estimate=FREE,
        name="powers",
    )(here, *[resident(p) for p in parts], resident(ct), *([outside(classes)] if first else [resident(b) for b in aliased]))


def place_of(order, rows_here, me, block, within):
    relative = block ^ me
    place = jnp.zeros_like(block)
    for i, b in enumerate(order):
        place = jnp.where(relative == b, i * rows_here, place)
    return place + within


def prepare_kernel(order, total_rows, here_ref, table_ref, requests_hbm, near_hbm, weight_hbm, e_hbm, c_hbm, *refs):
    whi_ref, wlo_ref, scale_ref, asked_ref, pick_ref, own_ref, ct_ref, row_ref, near_ref, weight_ref, requests_ref, sems = refs
    me = here_ref[2]
    peers, cap = requests_hbm.shape
    k, rows_here = near_hbm.shape
    depth = e_hbm.shape[1]
    split_at = streamed_from(c_hbm.shape[0])
    moves = (
        (requests_hbm, requests_ref),
        (near_hbm, near_ref),
        (weight_hbm, weight_ref),
        (e_hbm, own_ref.at[:, :depth]),
        (c_hbm.at[:split_at, :], ct_ref.at[:split_at, :]),
    )
    copies = [pltpu.make_async_copy(src, dst, sems.at[i]) for i, (src, dst) in enumerate(moves)]
    for copy in copies:
        copy.start()
    own_ref[:, depth:] = table_ref[...]
    row_ref[...] = jnp.full_like(row_ref, -1)
    for copy in copies[:3]:
        copy.wait()
    lane = lax.broadcasted_iota(jnp.int32, (1, LANES), 1)
    for p in range(peers):
        start = place_of(order, rows_here, me, jnp.full((1, 1), p, jnp.int32), 0)
        row = jnp.full((1, LANES), -1, jnp.int32)
        for j in range(cap):
            row = jnp.where(lane == j, requests_ref[p, j], row)
        row_ref[p : p + 1, :] = jnp.where(row >= 0, row + start, -1)
    asked = row_ref[...].T
    column = lax.broadcasted_iota(jnp.int32, (cap, total_rows), 1)
    for p in range(peers):
        one = asked[:cap, p : p + 1]
        asked_ref[p * cap : (p + 1) * cap, :] = jnp.broadcast_to(one, (cap, LANES))
        pick_ref[p * cap : (p + 1) * cap, :] = jnp.where(column == one, 1.0, 0.0).astype(bf16)

    near, weight = near_ref[...].T, weight_ref[...].T
    column = lax.broadcasted_iota(jnp.int32, whi_ref.shape, 1)
    acc = jnp.zeros(whi_ref.shape, f32)
    for i in range(k):
        acc = acc + jnp.where(column == near[:, i : i + 1], SMOOTHING * weight[:, i : i + 1], 0.0)
    scale = 1.0 / (1.0 + SMOOTHING * jnp.sum(weight, axis=1, keepdims=True))
    whi_ref[...], wlo_ref[...] = split(acc * scale)
    scale_ref[...] = jnp.broadcast_to(scale, scale_ref.shape)
    for copy in copies[3:]:
        copy.wait()


def prepared(here, table, requests, neighbours, weights, embeddings, classes, order, total_rows):
    rows_here, depth = embeddings.shape
    width = classes.shape[0]
    k = neighbours.shape[1]
    extended = rows_here + requests.size
    return pl.pallas_call(
        functools.partial(prepare_kernel, order, total_rows),
        in_specs=[SCALARS, WHOLE] + [HBM] * 5,
        out_specs=[WHOLE] * 7,
        out_shape=[
            VMEM((rows_here, extended), bf16),
            VMEM((rows_here, extended), bf16),
            VMEM((rows_here, LANES), f32),
            VMEM((requests.size, LANES), jnp.int32),
            VMEM((requests.size, total_rows), bf16),
            VMEM((rows_here, depth + LANES), bf16),
            VMEM((width, depth), bf16),
        ],
        scratch_shapes=[
            VMEM((LANES, LANES), jnp.int32),
            VMEM((k, rows_here), jnp.int32),
            VMEM((k, rows_here), f32),
            pltpu.SMEM(requests.shape, jnp.int32),
            pltpu.SemaphoreType.DMA((5,)),
        ],
        compiler_params=pltpu.CompilerParams(vmem_limit_bytes=(2 if total_rows <= 768 else 8) * MIB),
        cost_estimate=FREE,
        name="prepare",
    )(here, resident(table), *[outside(x) for x in (requests, neighbours.T, weights.T, embeddings, classes)])


def graph_kernel(order, k, here_ref, whi_ref, wlo_ref, scale_ref, asked_ref, pick_ref, tab_ref, m_ref, rows_ref, thi_ref, tlo_ref):
    me = here_ref[2]
    total_rows = tab_ref.shape[0]
    rows_here, extended = whi_ref.shape
    slots = round_up(k, 8)
    rows_ref[:rows_here, :] = tab_ref[:rows_here, :]
    rows_ref[rows_here:, :] = dot(pick_ref[...], tab_ref[...].astype(bf16))
    column = lax.broadcasted_iota(jnp.int32, (GROUP, total_rows), 1)
    sub = lax.broadcasted_iota(jnp.int32, (GROUP, LANES), 0)
    for start in range(0, extended, GROUP):
        tab = rows_ref[start : start + GROUP, :]
        within = pltpu.roll(tab, LANES - slots, 1).astype(jnp.int32)
        weight = pltpu.roll(tab, LANES - 2 * slots, 1) + pltpu.roll(tab, LANES - 3 * slots, 1) + pltpu.roll(tab, LANES - 4 * slots, 1)
        place = place_of(order, rows_here, me, tab.astype(jnp.int32), within)
        itself = sub + start if start < rows_here else asked_ref[start - rows_here : start - rows_here + GROUP, :]
        acc = jnp.where(column == itself[:, :1], 1.0, 0.0)
        degree = jnp.zeros((GROUP, 1), f32)
        for i in range(k):
            w = weight[:, i : i + 1]
            acc = acc + jnp.where(column == place[:, i : i + 1], SMOOTHING * w, 0.0)
            degree = degree + w
        thi_ref[start : start + GROUP, :], tlo_ref[start : start + GROUP, :] = split(acc * (1.0 / (1.0 + SMOOTHING * degree)))
    column = lax.broadcasted_iota(jnp.int32, (rows_here, total_rows), 1)
    sub = lax.broadcasted_iota(jnp.int32, (rows_here, total_rows), 0)
    own = jnp.where(column == sub, scale_ref[:, :1], 0.0)
    thi = thi_ref[...]
    m_ref[...] = own + dot(whi_ref[...], thi) + dot(wlo_ref[...], thi) + dot(whi_ref[...], tlo_ref[...])


def graph_of(here, edges, tab, order, k):
    total_rows = tab.shape[0]
    rows_here, extended = edges[0].shape
    return pl.pallas_call(
        functools.partial(graph_kernel, order, k),
        in_specs=[SCALARS] + [WHOLE] * 6,
        out_specs=WHOLE,
        out_shape=VMEM((rows_here, total_rows), f32),
        scratch_shapes=[VMEM((extended, LANES), f32), VMEM((extended, total_rows), bf16), VMEM((extended, total_rows), bf16)],
        compiler_params=pltpu.CompilerParams(vmem_limit_bytes=(6 if total_rows <= 768 else 20) * MIB),
        cost_estimate=FREE,
        name="graph",
    )(here, *[resident(x) for x in edges], resident(tab))


def apply_kernel(tiles, n_pieces, n_cls, m_ref, p_ref, *refs):
    tile_refs, top_refs, sum_refs = refs[:n_pieces], refs[n_pieces : 2 * n_pieces], refs[2 * n_pieces : 3 * n_pieces]
    far_refs = refs[3 * n_pieces : 3 * n_pieces + n_cls - 1]
    out_ref, _, staged, sems = refs[3 * n_pieces + n_cls - 1 :]
    rows_here = m_ref.shape[0]

    def row(pieces):
        return jnp.concatenate([p[...] for p in pieces], axis=1)

    tops = [row(top_refs)] + [r[0:1, :] for r in far_refs]
    sums = [row(sum_refs)] + [r[1:2, :] for r in far_refs]
    top = functools.reduce(jnp.maximum, tops)
    total = sum(s * jnp.exp(t - top) for s, t in zip(sums, tops))
    factors = jnp.exp(row(tile_refs) - top) / total
    copies = []
    for t, (a, b) in enumerate(tiles):
        whi, wlo = split(m_ref[...] * factors[t : t + 1, :])
        hi, lo = split(p_ref[:, a:b])
        x = dot(jnp.concatenate([whi, wlo], axis=0), hi)
        staged[:, a:b] = x[:rows_here] + x[rows_here:] + dot(whi, lo)
        copy = pltpu.make_async_copy(staged.at[:, a:b], out_ref.at[:, a:b], sems.at[t])
        copy.start()
        copies.append(copy)
    for copy in copies:
        copy.wait()


def applied(m, powers, tile_tops, tops, sums, far):
    rows_here, total_rows = m.shape
    width = powers.shape[1]
    tiles = column_tiles(width)
    operands = [m, powers, *tile_tops, *tops, *sums, *far]
    return pl.pallas_call(
        functools.partial(apply_kernel, tiles, len(tops), len(far) + 1),
        in_specs=[WHOLE] * len(operands),
        out_specs=[ANYWHERE, WHOLE],
        out_shape=[jax.ShapeDtypeStruct((rows_here, width), f32), VMEM(powers.shape, f32)],
        input_output_aliases={1: 1},
        scratch_shapes=[VMEM((rows_here, width), f32), pltpu.SemaphoreType.DMA((len(tiles),))],
        compiler_params=pltpu.CompilerParams(vmem_limit_bytes=(8 if total_rows <= 768 else 16) * MIB),
        cost_estimate=FREE,
        name="smooth",
    )(*[resident(x) for x in operands])[0]


def shards(n_img, n_cls, embeddings, class_text_embedding, neighbours, weights, requests):
    rows_here = embeddings.shape[0]
    width = class_text_embedding.shape[1]
    half = rows_here // 2
    me, col = lax.axis_index("img"), lax.axis_index("cls")
    total_rows = n_img * rows_here
    here = jnp.stack([jnp.minimum(LIVE - col * width, width), col & 1, me]).astype(jnp.int32)
    min_live = min(width, LIVE - (n_cls - 1) * width)

    classes = class_text_embedding.T
    mine, table = tables_of(here, requests[0], embeddings, neighbours, weights)
    first, relayed, before, beside, last = exchange_plan(n_img)
    order = [b for piece in before + beside + last for b in piece]

    def swap(x):
        return lax.ppermute(x, "cls", [(i, i ^ 1) for i in range(n_cls)])

    def exchange(x, step):
        return lax.ppermute(x, "img", [(i, i ^ step) for i in range(n_img)])

    def halves(x, blocks):
        other = swap(x)
        cuts = [slice(i * half, (i + 1) * half) for i in range(len(blocks))]
        return {b: [x[c], other[c]] for b, c in zip(blocks, cuts)}

    *edges, own, ct = prepared(here, table, requests[0], neighbours, weights, embeddings, classes, order, total_rows)
    buffers, first_row, tops, sums, tile_tops = None, 0, [], [], []

    def work(blocks):
        nonlocal ct, buffers, first_row
        parts = [x for b in blocks for x in pairs[b]]
        results = powers_of(parts, ct, classes, here, buffers, first_row, total_rows, min_live)
        if buffers is None:
            ct = results[5]
        buffers = results[:2]
        first_row += len(blocks) * rows_here
        tops.append(results[2])
        sums.append(results[3])
        tile_tops.append(results[4])

    pairs = {0: [own]}
    for piece in before:
        work(piece)
    held = [exchange(mine, b) for b in first]
    *held, tops[-1] = lax.optimization_barrier((*held, tops[-1]))
    got = exchange(jnp.concatenate([x for b, x in zip(first, held) if b in relayed], axis=0), 1)
    pairs |= halves(jnp.concatenate(held, axis=0), first)
    for piece in beside:
        work(piece)
    got, tops[-1] = lax.optimization_barrier((got, tops[-1]))
    pairs |= halves(got, [b ^ 1 for b in relayed])
    for piece in last:
        work(piece)
    powers, tab = buffers
    stats = jnp.concatenate([jnp.concatenate(tops, axis=1), jnp.concatenate(sums, axis=1)], axis=0)
    far = [lax.ppermute(stats, "cls", [(i, i ^ d) for i in range(n_cls)]) for d in range(1, n_cls)]
    m = graph_of(here, edges, tab, order, neighbours.shape[1])
    return applied(m, powers, tile_tops, tops, sums, far)


def solution(mesh):
    in_specs = (
        P("img", None),
        P(None, "cls"),
        P("img", None),
        P("img", None),
        P("img", None, None),
    )
    sizes = mesh.shape
    run = functools.partial(shards, sizes["img"], sizes["cls"])
    return jax.shard_map(run, mesh=mesh, in_specs=in_specs, out_specs=P("img", "cls"), check_vma=False)
```

```python
import functools
import jax
import jax.numpy as jnp
from jax import lax
from jax.experimental import pallas as pl
from jax.experimental.pallas import tpu as pltpu
from jax.sharding import PartitionSpec as P

LIVE = 21841
SMOOTHING = 1.0
TILE = 512
LANES = 128
HALF = LANES // 2
DEEP = 3
NT = (((1,), (1,)), ((), ()))
GROUP = 128
f32, bf16 = jnp.float32, jnp.bfloat16
VMEM = pltpu.VMEM
WHOLE = pl.BlockSpec(memory_space=VMEM)
SCALARS = pl.BlockSpec(memory_space=pltpu.SMEM)
ANYWHERE = pl.BlockSpec(memory_space=pl.ANY)
MIB = 2**20
FREE = pl.CostEstimate(flops=1000, bytes_accessed=1000, transcendentals=0)


def column_tiles(width):
    return [(a, min(a + TILE, width)) for a in range(0, width, TILE)]


def round_up(n, m):
    return -(-n // m) * m


def resident(x):
    return pltpu.with_memory_space_constraint(x, VMEM)


def exchange_plan(peers):
    direct = list(range(2, peers, 2))

    def cut(blocks):
        return [blocks[i : i + 4] for i in range(0, len(blocks), 4)]

    return [2] + direct[1:] + [3, 1], direct[1:], cut(direct + [1]), cut([3] + [b ^ 1 for b in direct[1:]])


def outside(x):
    return pltpu.with_memory_space_constraint(x, pltpu.HBM)


HBM = pl.BlockSpec(memory_space=pltpu.HBM)


def table_kernel(here_ref, requests_hbm, e_hbm, neighbours_hbm, weights_hbm, own_ref, mine_ref, table_ref, near_ref, weight_ref, requests_ref, sems):
    core, me = here_ref[1], here_ref[2]
    rows, depth = e_hbm.shape
    half = rows // 2
    peers, cap = requests_hbm.shape
    k = near_ref.shape[0]
    slots = round_up(k, 8)
    start = pl.multiple_of(core * half, 16)
    moves = (
        (requests_hbm, requests_ref),
        (neighbours_hbm, near_ref),
        (weights_hbm, weight_ref),
        (e_hbm.at[pl.ds(start, half), :], mine_ref.at[:, :depth]),
        (e_hbm, own_ref.at[:, :depth]),
    )
    copies = [pltpu.make_async_copy(src, dst, sems.at[i]) for i, (src, dst) in enumerate(moves)]
    for copy in copies:
        copy.start()
    table_ref[...] = jnp.zeros_like(table_ref)
    for copy in copies[:3]:
        copy.wait()
    near = near_ref[...]
    slot = near - rows
    block = jnp.zeros_like(near) + me
    within = near
    for p in range(peers):
        block = jnp.where(slot >= p * cap, p, block)
        for j in range(cap):
            within = jnp.where(slot == p * cap + j, requests_ref[p, j], within)
    weight = weight_ref[...]
    w0 = weight.astype(bf16).astype(f32)
    w1 = (weight - w0).astype(bf16).astype(f32)
    w2 = weight - w0 - w1
    for i, x in enumerate((block.astype(f32), within.astype(f32), w0, w1, w2)):
        table_ref[i * slots : i * slots + k, :] = x
    own_ref[:, depth:] = table_ref[...].T.astype(bf16)
    mine_ref[:, depth:] = own_ref[pl.ds(start, half), depth:]
    for copy in copies[3:]:
        copy.wait()


def tables_of(here, requests, embeddings, neighbours, weights):
    rows, depth = embeddings.shape
    k = neighbours.shape[1]
    return pl.pallas_call(
        table_kernel,
        in_specs=[SCALARS] + [HBM] * 4,
        out_specs=[WHOLE] * 2,
        out_shape=[VMEM((rows, depth + LANES), bf16), VMEM((rows // 2, depth + LANES), bf16)],
        scratch_shapes=[
            VMEM((LANES, rows), f32),
            VMEM((k, rows), jnp.int32),
            VMEM((k, rows), f32),
            pltpu.SMEM(requests.shape, jnp.int32),
            pltpu.SemaphoreType.DMA((5,)),
        ],
        compiler_params=pltpu.CompilerParams(vmem_limit_bytes=MIB),
        cost_estimate=pl.CostEstimate(flops=3 * 10**10, bytes_accessed=10**8, transcendentals=0),
        name="tables",
    )(here, outside(requests), outside(embeddings), outside(neighbours.T), outside(weights.T))


def split(x):
    hi = x.astype(bf16)
    return hi, (x - hi.astype(f32)).astype(bf16)


def dot(a, b):
    return jnp.dot(a, b, preferred_element_type=f32)


def add_powers(tiles, min_live, here_ref, e_ref, ct_ref, p_ref, rows, stat_ref, before=None):
    n = e_ref.shape[0]
    lane = lax.broadcasted_iota(jnp.int32, (n, LANES), 1)
    stat = jnp.where(lane < HALF, -1e30, 0.0)
    for t, (a, b) in enumerate(tiles):
        if before:
            before(t)
        logits = lax.dot_general(e_ref[...], ct_ref[a:b, :], NT, preferred_element_type=f32)
        if b > min_live:
            live = lax.broadcasted_iota(jnp.int32, logits.shape, 1) + a < here_ref[0]
            logits = jnp.where(live, logits, -1e30)
        top = jnp.max(logits, axis=1, keepdims=True)
        powers = jnp.exp(logits - top)
        if b > min_live:
            powers = jnp.where(live, powers, 0.0)
        p_ref[rows, a:b] = powers
        stat = jnp.where(lane == t, top, stat)
        stat = jnp.where(lane == t + HALF, jnp.sum(powers, axis=1, keepdims=True), stat)
    stat_ref[rows, :] = stat
    return stat


def row_stats(stat, slots):
    turned = stat.T
    tops, sums = turned[:slots], turned[HALF : HALF + slots]
    top = jnp.max(tops, axis=0, keepdims=True)
    return tops, jnp.concatenate([top, jnp.sum(sums * jnp.exp(tops - top), axis=0, keepdims=True)], axis=0)


def powers_kernel(tiles, min_live, depth, first_row, n_parts, final, here_ref, *refs):
    parts, ct_ref = refs[:n_parts], refs[n_parts]
    p_ref, tab_ref, stat_ref, *ends, e_ref = refs[n_parts + 4 :]
    if final:
        tile_ref, both_ref = ends
        slots = tile_ref.shape[0]
        tops, both = row_stats(stat_ref[:first_row, :], slots)
    core = here_ref[1]
    row = 0
    for i, part in enumerate(parts):
        n = part.shape[0]
        at = pl.multiple_of(row + n * (-core if i % 2 else core), 16)
        e_ref[pl.ds(at, n), :] = part[:, :depth]
        tab_ref[pl.ds(first_row + at, n), :] = part[:, depth:].astype(f32)
        row += n
    stat = add_powers(tiles, min_live, here_ref, e_ref, ct_ref, p_ref, slice(first_row, first_row + row), stat_ref)
    if final:
        own_tops, own_both = row_stats(stat, slots)
        tile_ref[...] = jnp.concatenate([tops, own_tops], axis=1)
        both_ref[...] = jnp.concatenate([both, own_both], axis=1)


def powers_shapes(total_rows, width):
    return [VMEM((total_rows, width), f32), VMEM((total_rows, LANES), f32), VMEM((total_rows, LANES), f32)]


def powers_of(parts, ct, here, buffers, first_row, min_live):
    width, depth = ct.shape
    rows = sum(p.shape[0] for p in parts)
    total_rows = buffers[0].shape[0]
    tiles = column_tiles(width)
    final = first_row + rows == total_rows
    n = len(parts)
    shapes = powers_shapes(total_rows, width)
    if final:
        shapes += [VMEM((round_up(len(tiles), 8), total_rows), f32), VMEM((2, total_rows), f32)]
    return pl.pallas_call(
        functools.partial(powers_kernel, tiles, min_live, depth, first_row, n, final),
        in_specs=[SCALARS] + [WHOLE] * (n + 4),
        out_specs=[WHOLE] * len(shapes),
        out_shape=shapes,
        scratch_shapes=[VMEM((rows, depth), bf16)],
        input_output_aliases={2 + n + i: i for i in range(3)},
        compiler_params=pltpu.CompilerParams(vmem_limit_bytes=8 * MIB),
        cost_estimate=FREE,
        name="powers",
    )(here, *[resident(x) for x in parts], ct, *[resident(x) for x in buffers])


def place_of(order, rows_here, me, block, within):
    relative = block ^ me
    place = jnp.zeros_like(block)
    for i, b in enumerate(order):
        place = jnp.where(relative == b, i * rows_here, place)
    return place + within


def own_kernel(tiles, min_live, order, here_ref, own_ref, ct_ref, requests_hbm, near_hbm, weight_hbm, *refs):
    p_ref, tab_ref, stat_ref, whi_ref, wlo_ref, scale_ref, asked_ref, pick_ref = refs[:8]
    e_ref, row_ref, near_ref, weight_ref, requests_ref, sems = refs[8:]
    me = here_ref[2]
    peers, cap = requests_hbm.shape
    k, rows_here = near_hbm.shape
    total_rows = tab_ref.shape[0]
    moves = (
        (requests_hbm, requests_ref),
        (near_hbm, near_ref),
        (weight_hbm, weight_ref),
    )
    copies = [pltpu.make_async_copy(src, dst, sems.at[i]) for i, (src, dst) in enumerate(moves)]
    for copy in copies:
        copy.start()
    depth = e_ref.shape[1]
    e_ref[...] = own_ref[:, :depth]
    tab_ref[:rows_here, :] = own_ref[:, depth:].astype(f32)
    row_ref[...] = jnp.full_like(row_ref, -1)
    for copy in copies:
        copy.wait()

    def edges():
        lane = lax.broadcasted_iota(jnp.int32, (1, LANES), 1)
        for p in range(peers):
            start = place_of(order, rows_here, me, jnp.full((1, 1), p, jnp.int32), 0)
            row = jnp.full((1, LANES), -1, jnp.int32)
            for j in range(cap):
                row = jnp.where(lane == j, requests_ref[p, j], row)
            row_ref[p : p + 1, :] = jnp.where(row >= 0, row + start, -1)
        asked = row_ref[...].T
        column = lax.broadcasted_iota(jnp.int32, (cap, total_rows), 1)
        for p in range(peers):
            one = asked[:cap, p : p + 1]
            asked_ref[p * cap : (p + 1) * cap, :] = jnp.broadcast_to(one, (cap, LANES))
            pick_ref[p * cap : (p + 1) * cap, :] = jnp.where(column == one, 1.0, 0.0).astype(bf16)
        near, weight = near_ref[...].T, weight_ref[...].T
        column = lax.broadcasted_iota(jnp.int32, whi_ref.shape, 1)
        acc = jnp.zeros(whi_ref.shape, f32)
        for i in range(k):
            acc = acc + jnp.where(column == near[:, i : i + 1], SMOOTHING * weight[:, i : i + 1], 0.0)
        scale = 1.0 / (1.0 + SMOOTHING * jnp.sum(weight, axis=1, keepdims=True))
        whi_ref[...], wlo_ref[...] = split(acc * scale)
        scale_ref[...] = jnp.broadcast_to(scale, scale_ref.shape)

    edges()
    add_powers(tiles, min_live, here_ref, e_ref, ct_ref, p_ref, slice(0, rows_here), stat_ref)


def own_powers(here, own, requests, neighbours, weights, classes, order, total_rows, min_live):
    rows_here = own.shape[0]
    width, depth = classes.shape
    k = neighbours.shape[1]
    extended = rows_here + requests.size
    tiles = column_tiles(width)
    shapes = powers_shapes(total_rows, width) + [
        VMEM((rows_here, extended), bf16),
        VMEM((rows_here, extended), bf16),
        VMEM((rows_here, LANES), f32),
        VMEM((requests.size, LANES), jnp.int32),
        VMEM((requests.size, total_rows), bf16),
    ]
    return pl.pallas_call(
        functools.partial(own_kernel, tiles, min_live, order),
        in_specs=[SCALARS, WHOLE, WHOLE] + [HBM] * 3,
        out_specs=[WHOLE] * len(shapes),
        out_shape=shapes,
        scratch_shapes=[
            VMEM((rows_here, depth), bf16),
            VMEM((LANES, LANES), jnp.int32),
            VMEM((k, rows_here), jnp.int32),
            VMEM((k, rows_here), f32),
            pltpu.SMEM(requests.shape, jnp.int32),
            pltpu.SemaphoreType.DMA((3,)),
        ],
        compiler_params=pltpu.CompilerParams(vmem_limit_bytes=8 * MIB),
        cost_estimate=FREE,
        name="own",
    )(here, resident(own), classes, *[outside(x) for x in (requests, neighbours.T, weights.T)])


def spans(rows_here, extended):
    return [(0, rows_here)] + [(a, min(GROUP, extended - a)) for a in range(rows_here, extended, GROUP)]


def graph_kernel(order, k, here_ref, whi_ref, wlo_ref, scale_ref, asked_ref, pick_ref, tab_ref, m_ref, rows_ref, thi_ref, tlo_ref):
    me = here_ref[2]
    total_rows = tab_ref.shape[0]
    rows_here, extended = whi_ref.shape
    slots = round_up(k, 8)
    rows_ref[rows_here:, :] = dot(pick_ref[...], tab_ref[...].astype(bf16))
    for start, size in spans(rows_here, extended):
        column = lax.broadcasted_iota(jnp.int32, (size, total_rows), 1)
        tab = tab_ref[:rows_here, :] if start < rows_here else rows_ref[start : start + size, :]
        within = pltpu.roll(tab, LANES - slots, 1).astype(jnp.int32)
        weight = pltpu.roll(tab, LANES - 2 * slots, 1) + pltpu.roll(tab, LANES - 3 * slots, 1) + pltpu.roll(tab, LANES - 4 * slots, 1)
        place = place_of(order, rows_here, me, tab.astype(jnp.int32), within)
        itself = lax.broadcasted_iota(jnp.int32, (size, LANES), 0) if start < rows_here else asked_ref[start - rows_here : start - rows_here + size, :]
        acc = jnp.where(column == itself[:, :1], 1.0, 0.0)
        degree = jnp.zeros((size, 1), f32)
        for i in range(k):
            w = weight[:, i : i + 1]
            acc = acc + jnp.where(column == place[:, i : i + 1], SMOOTHING * w, 0.0)
            degree = degree + w
        thi_ref[start : start + size, :], tlo_ref[start : start + size, :] = split(acc * (1.0 / (1.0 + SMOOTHING * degree)))
    column = lax.broadcasted_iota(jnp.int32, (rows_here, total_rows), 1)
    sub = lax.broadcasted_iota(jnp.int32, (rows_here, total_rows), 0)
    own = jnp.where(column == sub, scale_ref[:, :1], 0.0)
    thi = thi_ref[...]
    m_ref[...] = own + dot(whi_ref[...], thi) + dot(wlo_ref[...], thi) + dot(whi_ref[...], tlo_ref[...])


def graph_of(here, edges, tab, order, k):
    total_rows = tab.shape[0]
    rows_here, extended = edges[0].shape
    return pl.pallas_call(
        functools.partial(graph_kernel, order, k),
        in_specs=[SCALARS] + [WHOLE] * 6,
        out_specs=WHOLE,
        out_shape=VMEM((rows_here, total_rows), f32),
        scratch_shapes=[VMEM((extended, LANES), f32), VMEM((extended, total_rows), bf16), VMEM((extended, total_rows), bf16)],
        compiler_params=pltpu.CompilerParams(vmem_limit_bytes=(6 if total_rows <= 768 else 20) * MIB),
        cost_estimate=FREE,
        name="graph",
    )(here, *[resident(x) for x in edges], resident(tab))


def apply_kernel(tiles, m_ref, p_ref, tile_ref, *refs):
    *stat_refs, out_ref, _, staged, sems = refs
    rows_here = m_ref.shape[0]
    tops, sums = [r[0:1, :] for r in stat_refs], [r[1:2, :] for r in stat_refs]
    top = functools.reduce(jnp.maximum, tops)
    total = sum(s * jnp.exp(t - top) for s, t in zip(sums, tops))
    factors = jnp.exp(tile_ref[...] - top) / total
    copies = []
    for t, (a, b) in enumerate(tiles):
        whi, wlo = split(m_ref[...] * factors[t : t + 1, :])
        hi, lo = split(p_ref[:, a:b])
        x = dot(jnp.concatenate([whi, wlo], axis=0), hi)
        staged[:, a:b] = x[:rows_here] + x[rows_here:] + dot(whi, lo)
        copy = pltpu.make_async_copy(staged.at[:, a:b], out_ref.at[:, a:b], sems.at[t])
        copy.start()
        copies.append(copy)
    for copy in copies:
        copy.wait()


def applied(m, powers, tile_tops, stats, far):
    rows_here, width = m.shape[0], powers.shape[1]
    total_rows = m.shape[1]
    tiles = column_tiles(width)
    operands = [m, powers, tile_tops, stats, *far]
    return pl.pallas_call(
        functools.partial(apply_kernel, tiles),
        in_specs=[WHOLE] * len(operands),
        out_specs=[ANYWHERE, WHOLE],
        out_shape=[jax.ShapeDtypeStruct((rows_here, width), f32), VMEM(powers.shape, f32)],
        input_output_aliases={1: 1},
        scratch_shapes=[VMEM((rows_here, width), f32), pltpu.SemaphoreType.DMA((len(tiles),))],
        compiler_params=pltpu.CompilerParams(vmem_limit_bytes=(8 if total_rows <= 768 else 16) * MIB),
        cost_estimate=FREE,
        name="smooth",
    )(*[resident(x) for x in operands])[0]


def shards(n_img, n_cls, embeddings, class_text_embedding, neighbours, weights, requests):
    rows_here = embeddings.shape[0]
    width = class_text_embedding.shape[1]
    half = rows_here // 2
    me, col = lax.axis_index("img"), lax.axis_index("cls")
    total_rows = n_img * rows_here
    here = jnp.stack([jnp.minimum(LIVE - col * width, width), col & 1, me]).astype(jnp.int32)
    min_live = min(width, LIVE - (n_cls - 1) * width)

    classes = class_text_embedding.T
    own, mine = tables_of(here, requests[0], embeddings, neighbours, weights)
    first, relayed, beside, last = exchange_plan(n_img)
    order = [0] + [b for piece in beside + last for b in piece]

    def swap(x):
        return lax.ppermute(x, "cls", [(i, i ^ 1) for i in range(n_cls)])

    def exchange(x, step):
        return lax.ppermute(x, "img", [(i, i ^ step) for i in range(n_img)])

    def halves(x, blocks):
        other = swap(x)
        cuts = [slice(i * half, (i + 1) * half) for i in range(len(blocks))]
        return {b: [x[c], other[c]] for b, c in zip(blocks, cuts)}

    held = [exchange(mine, b) for b in first]
    results = own_powers(here, own, requests[0], neighbours, weights, classes, order, total_rows, min_live)
    buffers, first_row, edges = list(results[:3]), rows_here, results[3:]

    def work(blocks):
        nonlocal buffers, first_row
        parts = [x for b in blocks for x in pairs[b]]
        buffers = list(powers_of(parts, classes, here, buffers, first_row, min_live))
        first_row += len(blocks) * rows_here

    *held, buffers[2] = lax.optimization_barrier((*held, buffers[2]))
    got = exchange(jnp.concatenate([x for b, x in zip(first, held) if b in relayed], axis=0), 1)
    pairs = halves(jnp.concatenate(held, axis=0), first)
    for piece in beside:
        work(piece)
    got, buffers[2] = lax.optimization_barrier((got, buffers[2]))
    pairs |= halves(got, [b ^ 1 for b in relayed])
    for piece in last:
        work(piece)
    powers, tab, _, tile_tops, stats = buffers
    far = [lax.ppermute(stats, "cls", [(i, i ^ d) for i in range(n_cls)]) for d in range(1, n_cls)]
    m = graph_of(here, edges, tab, order, neighbours.shape[1])
    return applied(m, powers, tile_tops, stats, far)


def solution(mesh):
    in_specs = (
        P("img", None),
        P(None, "cls"),
        P("img", None),
        P("img", None),
        P("img", None, None),
    )
    sizes = mesh.shape
    run = functools.partial(shards, sizes["img"], sizes["cls"])
    return jax.shard_map(run, mesh=mesh, in_specs=in_specs, out_specs=P("img", "cls"), check_vma=False)
```

```python
import functools
import jax
import jax.numpy as jnp
from jax import lax
from jax.experimental import pallas as pl
from jax.experimental.pallas import tpu as pltpu
from jax.sharding import PartitionSpec as P

LIVE = 21841
SMOOTHING = 1.0
TILE = 512
LANES = 128
HALF = LANES // 2
DEEP = 3
NT = (((1,), (1,)), ((), ()))
GROUP = 128
f32, bf16 = jnp.float32, jnp.bfloat16
VMEM = pltpu.VMEM
WHOLE = pl.BlockSpec(memory_space=VMEM)
SCALARS = pl.BlockSpec(memory_space=pltpu.SMEM)
ANYWHERE = pl.BlockSpec(memory_space=pl.ANY)
MIB = 2**20
FREE = pl.CostEstimate(flops=1000, bytes_accessed=1000, transcendentals=0)


def column_tiles(width):
    return [(a, min(a + TILE, width)) for a in range(0, width, TILE)]


def round_up(n, m):
    return -(-n // m) * m


def resident(x):
    return pltpu.with_memory_space_constraint(x, VMEM)


def exchange_plan(peers):
    direct = list(range(2, peers, 2))

    def cut(blocks):
        return [blocks[i : i + 4] for i in range(0, len(blocks), 4)]

    return [2] + direct[1:] + [3, 1], direct[1:], cut(direct + [1]), cut([3] + [b ^ 1 for b in direct[1:]])


def outside(x):
    return pltpu.with_memory_space_constraint(x, pltpu.HBM)


HBM = pl.BlockSpec(memory_space=pltpu.HBM)


def table_kernel(here_ref, requests_hbm, e_hbm, neighbours_hbm, weights_hbm, mine_ref, out_ref, table_ref, near_ref, weight_ref, requests_ref, sems):
    core, me = here_ref[1], here_ref[2]
    rows, depth = e_hbm.shape
    half = rows // 2
    peers, cap = requests_hbm.shape
    k = near_ref.shape[0]
    slots = round_up(k, 8)
    start = pl.multiple_of(core * half, 16)
    moves = (
        (requests_hbm, requests_ref),
        (neighbours_hbm, near_ref),
        (weights_hbm, weight_ref),
        (e_hbm.at[pl.ds(start, half), :], mine_ref.at[:, :depth]),
    )
    copies = [pltpu.make_async_copy(src, dst, sems.at[i]) for i, (src, dst) in enumerate(moves)]
    for copy in copies:
        copy.start()
    table_ref[...] = jnp.zeros_like(table_ref)
    for copy in copies[:3]:
        copy.wait()
    near = near_ref[...]
    slot = near - rows
    block = jnp.zeros_like(near) + me
    within = near
    for p in range(peers):
        block = jnp.where(slot >= p * cap, p, block)
        for j in range(cap):
            within = jnp.where(slot == p * cap + j, requests_ref[p, j], within)
    weight = weight_ref[...]
    w0 = weight.astype(bf16).astype(f32)
    w1 = (weight - w0).astype(bf16).astype(f32)
    w2 = weight - w0 - w1
    for i, x in enumerate((block.astype(f32), within.astype(f32), w0, w1, w2)):
        table_ref[i * slots : i * slots + k, :] = x
    out_ref[...] = table_ref[...].T.astype(bf16)
    mine_ref[:, depth:] = out_ref[pl.ds(start, half), :]
    copies[3].wait()


def tables_of(here, requests, embeddings, neighbours, weights):
    rows, depth = embeddings.shape
    k = neighbours.shape[1]
    return pl.pallas_call(
        table_kernel,
        in_specs=[SCALARS] + [HBM] * 4,
        out_specs=[WHOLE] * 2,
        out_shape=[VMEM((rows // 2, depth + LANES), bf16), VMEM((rows, LANES), bf16)],
        scratch_shapes=[
            VMEM((LANES, rows), f32),
            VMEM((k, rows), jnp.int32),
            VMEM((k, rows), f32),
            pltpu.SMEM(requests.shape, jnp.int32),
            pltpu.SemaphoreType.DMA((4,)),
        ],
        compiler_params=pltpu.CompilerParams(vmem_limit_bytes=MIB),
        cost_estimate=pl.CostEstimate(flops=3 * 10**10, bytes_accessed=10**8, transcendentals=0),
        name="tables",
    )(here, outside(requests), outside(embeddings), outside(neighbours.T), outside(weights.T))


def split(x):
    hi = x.astype(bf16)
    return hi, (x - hi.astype(f32)).astype(bf16)


def dot(a, b):
    return jnp.dot(a, b, preferred_element_type=f32)


def add_powers(tiles, min_live, here_ref, e_ref, ct_ref, p_ref, rows, stat_ref, before=None):
    n = e_ref.shape[0]
    lane = lax.broadcasted_iota(jnp.int32, (n, LANES), 1)
    stat = jnp.where(lane < HALF, -1e30, 0.0)
    for t, (a, b) in enumerate(tiles):
        if before:
            before(t)
        logits = lax.dot_general(e_ref[...], ct_ref[a:b, :], NT, preferred_element_type=f32)
        if b > min_live:
            live = lax.broadcasted_iota(jnp.int32, logits.shape, 1) + a < here_ref[0]
            logits = jnp.where(live, logits, -1e30)
        top = jnp.max(logits, axis=1, keepdims=True)
        powers = jnp.exp(logits - top)
        if b > min_live:
            powers = jnp.where(live, powers, 0.0)
        p_ref[rows, a:b] = powers
        stat = jnp.where(lane == t, top, stat)
        stat = jnp.where(lane == t + HALF, jnp.sum(powers, axis=1, keepdims=True), stat)
    stat_ref[rows, :] = stat
    return stat


def row_stats(stat, slots):
    turned = stat.T
    tops, sums = turned[:slots], turned[HALF : HALF + slots]
    top = jnp.max(tops, axis=0, keepdims=True)
    return tops, jnp.concatenate([top, jnp.sum(sums * jnp.exp(tops - top), axis=0, keepdims=True)], axis=0)


def powers_kernel(tiles, min_live, depth, first_row, n_parts, final, here_ref, *refs):
    parts, ct_ref = refs[:n_parts], refs[n_parts]
    p_ref, tab_ref, stat_ref, *ends, e_ref = refs[n_parts + 4 :]
    if final:
        tile_ref, both_ref = ends
        slots = tile_ref.shape[0]
        tops, both = row_stats(stat_ref[:first_row, :], slots)
    core = here_ref[1]
    row = 0
    for i, part in enumerate(parts):
        n = part.shape[0]
        at = pl.multiple_of(row + n * (-core if i % 2 else core), 16)
        e_ref[pl.ds(at, n), :] = part[:, :depth]
        tab_ref[pl.ds(first_row + at, n), :] = part[:, depth:].astype(f32)
        row += n
    stat = add_powers(tiles, min_live, here_ref, e_ref, ct_ref, p_ref, slice(first_row, first_row + row), stat_ref)
    if final:
        own_tops, own_both = row_stats(stat, slots)
        tile_ref[...] = jnp.concatenate([tops, own_tops], axis=1)
        both_ref[...] = jnp.concatenate([both, own_both], axis=1)


def powers_shapes(total_rows, width):
    return [VMEM((total_rows, width), f32), VMEM((total_rows, LANES), f32), VMEM((total_rows, LANES), f32)]


def powers_of(parts, ct, here, buffers, first_row, min_live):
    width, depth = ct.shape
    rows = sum(p.shape[0] for p in parts)
    total_rows = buffers[0].shape[0]
    tiles = column_tiles(width)
    final = first_row + rows == total_rows
    n = len(parts)
    shapes = powers_shapes(total_rows, width)
    if final:
        shapes += [VMEM((round_up(len(tiles), 8), total_rows), f32), VMEM((2, total_rows), f32)]
    return pl.pallas_call(
        functools.partial(powers_kernel, tiles, min_live, depth, first_row, n, final),
        in_specs=[SCALARS] + [WHOLE] * (n + 4),
        out_specs=[WHOLE] * len(shapes),
        out_shape=shapes,
        scratch_shapes=[VMEM((rows, depth), bf16)],
        input_output_aliases={2 + n + i: i for i in range(3)},
        compiler_params=pltpu.CompilerParams(vmem_limit_bytes=8 * MIB),
        cost_estimate=FREE,
        name="powers",
    )(here, *[resident(x) for x in parts], ct, *[resident(x) for x in buffers])


def place_of(order, rows_here, me, block, within):
    relative = block ^ me
    place = jnp.zeros_like(block)
    for i, b in enumerate(order):
        place = jnp.where(relative == b, i * rows_here, place)
    return place + within


def second_rows(order, rows_here, me, k, tab, itself, total_rows):
    n, slots = tab.shape[0], round_up(k, 8)
    within = pltpu.roll(tab, LANES - slots, 1).astype(jnp.int32)
    weight = pltpu.roll(tab, LANES - 2 * slots, 1) + pltpu.roll(tab, LANES - 3 * slots, 1) + pltpu.roll(tab, LANES - 4 * slots, 1)
    place = place_of(order, rows_here, me, tab.astype(jnp.int32), within)
    column = lax.broadcasted_iota(jnp.int32, (n, total_rows), 1)
    acc = jnp.where(column == itself, 1.0, 0.0)
    degree = jnp.zeros((n, 1), f32)
    for i in range(k):
        w = weight[:, i : i + 1]
        acc = acc + jnp.where(column == place[:, i : i + 1], SMOOTHING * w, 0.0)
        degree = degree + w
    return split(acc * (1.0 / (1.0 + SMOOTHING * degree)))


def own_kernel(tiles, min_live, order, here_ref, table_ref, own_ref, ct_ref, requests_hbm, near_hbm, weight_hbm, *refs):
    p_ref, tab_ref, stat_ref, m_ref, whi_ref, wlo_ref, asked_ref, pick_ref = refs[:8]
    row_ref, near_ref, weight_ref, requests_ref, sems = refs[8:]
    me = here_ref[2]
    peers, cap = requests_hbm.shape
    k, rows_here = near_hbm.shape
    total_rows = tab_ref.shape[0]
    moves = (
        (requests_hbm, requests_ref),
        (near_hbm, near_ref),
        (weight_hbm, weight_ref),
    )
    copies = [pltpu.make_async_copy(src, dst, sems.at[i]) for i, (src, dst) in enumerate(moves)]
    for copy in copies:
        copy.start()
    tab = table_ref[...].astype(f32)
    tab_ref[:rows_here, :] = tab
    row_ref[...] = jnp.full_like(row_ref, -1)
    for copy in copies:
        copy.wait()

    lane = lax.broadcasted_iota(jnp.int32, (1, LANES), 1)
    for p in range(peers):
        start = place_of(order, rows_here, me, jnp.full((1, 1), p, jnp.int32), 0)
        row = jnp.full((1, LANES), -1, jnp.int32)
        for j in range(cap):
            row = jnp.where(lane == j, requests_ref[p, j], row)
        row_ref[p : p + 1, :] = jnp.where(row >= 0, row + start, -1)
    asked = row_ref[...].T
    column = lax.broadcasted_iota(jnp.int32, (cap, total_rows), 1)
    for p in range(peers):
        one = asked[:cap, p : p + 1]
        asked_ref[p * cap : (p + 1) * cap, :] = jnp.broadcast_to(one, (cap, LANES))
        pick_ref[p * cap : (p + 1) * cap, :] = jnp.where(column == one, 1.0, 0.0).astype(bf16)

    near, weight = near_ref[...].T, weight_ref[...].T
    scale = 1.0 / (1.0 + SMOOTHING * jnp.sum(weight, axis=1, keepdims=True))

    def edges(offset, n):
        column = lax.broadcasted_iota(jnp.int32, (rows_here, n), 1) + offset
        acc = jnp.zeros((rows_here, n), f32)
        for i in range(k):
            acc = acc + jnp.where(column == near[:, i : i + 1], SMOOTHING * weight[:, i : i + 1], 0.0)
        return split(acc * scale)

    whi_ref[...], wlo_ref[...] = edges(rows_here, whi_ref.shape[1])
    whi, wlo = edges(0, rows_here)
    itself = lax.broadcasted_iota(jnp.int32, (rows_here, 1), 0)
    thi, tlo = second_rows(order, rows_here, me, k, tab, itself, total_rows)
    own = jnp.where(lax.broadcasted_iota(jnp.int32, (rows_here, total_rows), 1) == itself, scale, 0.0)
    m_ref[...] = own + dot(whi, thi) + dot(wlo, thi) + dot(whi, tlo)
    add_powers(tiles, min_live, here_ref, own_ref, ct_ref, p_ref, slice(0, rows_here), stat_ref)


def own_powers(here, table, embeddings, requests, neighbours, weights, classes, order, total_rows, min_live):
    rows_here, k = neighbours.shape
    width = classes.shape[0]
    tiles = column_tiles(width)
    shapes = powers_shapes(total_rows, width) + [
        VMEM((rows_here, total_rows), f32),
        VMEM((rows_here, requests.size), bf16),
        VMEM((rows_here, requests.size), bf16),
        VMEM((requests.size, LANES), jnp.int32),
        VMEM((requests.size, total_rows), bf16),
    ]
    return pl.pallas_call(
        functools.partial(own_kernel, tiles, min_live, order),
        in_specs=[SCALARS] + [WHOLE] * 3 + [HBM] * 3,
        out_specs=[WHOLE] * len(shapes),
        out_shape=shapes,
        scratch_shapes=[
            VMEM((LANES, LANES), jnp.int32),
            VMEM((k, rows_here), jnp.int32),
            VMEM((k, rows_here), f32),
            pltpu.SMEM(requests.shape, jnp.int32),
            pltpu.SemaphoreType.DMA((3,)),
        ],
        compiler_params=pltpu.CompilerParams(vmem_limit_bytes=(8 if total_rows <= 768 else 14) * MIB),
        cost_estimate=FREE,
        name="own",
    )(here, resident(table), embeddings, classes, *[outside(x) for x in (requests, neighbours.T, weights.T)])


def graph_kernel(order, k, here_ref, m_ref, whi_ref, wlo_ref, asked_ref, pick_ref, tab_ref, out_ref):
    rows_here, total_rows = m_ref.shape
    asked = whi_ref.shape[1]
    tab = dot(pick_ref[...], tab_ref[...].astype(bf16))
    acc = m_ref[...]
    for start in range(0, asked, GROUP):
        rows = slice(start, min(start + GROUP, asked))
        thi, tlo = second_rows(order, rows_here, here_ref[2], k, tab[rows], asked_ref[rows, :1], total_rows)
        whi, wlo = whi_ref[:, rows], wlo_ref[:, rows]
        acc = acc + dot(whi, thi) + dot(wlo, thi) + dot(whi, tlo)
    out_ref[...] = acc


def graph_of(here, edges, tab, order, k):
    total_rows = tab.shape[0]
    return pl.pallas_call(
        functools.partial(graph_kernel, order, k),
        in_specs=[SCALARS] + [WHOLE] * 6,
        out_specs=WHOLE,
        out_shape=VMEM(edges[0].shape, f32),
        compiler_params=pltpu.CompilerParams(vmem_limit_bytes=(6 if total_rows <= 768 else 20) * MIB),
        cost_estimate=FREE,
        name="graph",
    )(here, *[resident(x) for x in edges], resident(tab))


def apply_kernel(tiles, m_ref, p_ref, tile_ref, *refs):
    *stat_refs, out_ref, _, staged, sems = refs
    rows_here = m_ref.shape[0]
    tops = [r[i : i + 1, :] for r in stat_refs for i in (0, 2)]
    sums = [r[i : i + 1, :] for r in stat_refs for i in (1, 3)]
    top = functools.reduce(jnp.maximum, tops)
    total = sum(s * jnp.exp(t - top) for s, t in zip(sums, tops))
    factors = jnp.exp(tile_ref[...] - top) / total
    copies = []
    for t, (a, b) in enumerate(tiles):
        whi, wlo = split(m_ref[...] * factors[t : t + 1, :])
        hi, lo = split(p_ref[:, a:b])
        x = dot(jnp.concatenate([whi, wlo], axis=0), hi)
        staged[:, a:b] = x[:rows_here] + x[rows_here:] + dot(whi, lo)
        copy = pltpu.make_async_copy(staged.at[:, a:b], out_ref.at[:, a:b], sems.at[t])
        copy.start()
        copies.append(copy)
    for copy in copies:
        copy.wait()


def applied(m, powers, tile_tops, stats):
    rows_here, width = m.shape[0], powers.shape[1]
    total_rows = m.shape[1]
    tiles = column_tiles(width)
    operands = [m, powers, tile_tops, *stats]
    return pl.pallas_call(
        functools.partial(apply_kernel, tiles),
        in_specs=[WHOLE] * len(operands),
        out_specs=[ANYWHERE, WHOLE],
        out_shape=[jax.ShapeDtypeStruct((rows_here, width), f32), VMEM(powers.shape, f32)],
        input_output_aliases={1: 1},
        scratch_shapes=[VMEM((rows_here, width), f32), pltpu.SemaphoreType.DMA((len(tiles),))],
        compiler_params=pltpu.CompilerParams(vmem_limit_bytes=(8 if total_rows <= 768 else 16) * MIB),
        cost_estimate=FREE,
        name="smooth",
    )(*[resident(x) for x in operands])[0]


def shards(n_img, n_cls, embeddings, class_text_embedding, neighbours, weights, requests):
    rows_here = embeddings.shape[0]
    width = class_text_embedding.shape[1]
    half = rows_here // 2
    me, col = lax.axis_index("img"), lax.axis_index("cls")
    total_rows = n_img * rows_here
    here = jnp.stack([jnp.minimum(LIVE - col * width, width), col & 1, me]).astype(jnp.int32)
    min_live = min(width, LIVE - (n_cls - 1) * width)

    classes = class_text_embedding.T
    mine, table = tables_of(here, requests[0], embeddings, neighbours, weights)
    first, relayed, beside, last = exchange_plan(n_img)
    order = [0] + [b for piece in beside + last for b in piece]

    def swap(x):
        return lax.ppermute(x, "cls", [(i, i ^ 1) for i in range(n_cls)])

    def exchange(x, step):
        return lax.ppermute(x, "img", [(i, i ^ step) for i in range(n_img)])

    def halves(x, blocks):
        other = swap(x)
        cuts = [slice(i * half, (i + 1) * half) for i in range(len(blocks))]
        return {b: [x[c], other[c]] for b, c in zip(blocks, cuts)}

    held = [exchange(mine, b) for b in first]
    results = own_powers(here, table, embeddings, requests[0], neighbours, weights, classes, order, total_rows, min_live)
    buffers, first_row, edges = list(results[:3]), rows_here, results[3:]

    def work(blocks):
        nonlocal buffers, first_row
        parts = [x for b in blocks for x in pairs[b]]
        buffers = list(powers_of(parts, classes, here, buffers, first_row, min_live))
        first_row += len(blocks) * rows_here

    *held, buffers[2] = lax.optimization_barrier((*held, buffers[2]))
    got = exchange(jnp.concatenate([x for b, x in zip(first, held) if b in relayed], axis=0), 1)
    pairs = halves(jnp.concatenate(held, axis=0), first)
    for piece in beside:
        work(piece)
    got, buffers[2] = lax.optimization_barrier((got, buffers[2]))
    pairs |= halves(got, [b ^ 1 for b in relayed])
    for piece in last:
        work(piece)
    powers, tab, _, tile_tops, stats = buffers
    stats = jnp.concatenate([stats, swap(stats)], axis=0)
    stats, tab = lax.optimization_barrier((stats, tab))
    far = [lax.ppermute(stats, "cls", [(i, i ^ d) for i in range(n_cls)]) for d in range(2, n_cls, 2)]
    m = graph_of(here, edges, tab, order, neighbours.shape[1])
    return applied(m, powers, tile_tops, [stats, *far])


def solution(mesh):
    in_specs = (
        P("img", None),
        P(None, "cls"),
        P("img", None),
        P("img", None),
        P("img", None, None),
    )
    sizes = mesh.shape
    run = functools.partial(shards, sizes["img"], sizes["cls"])
    return jax.shard_map(run, mesh=mesh, in_specs=in_specs, out_specs=P("img", "cls"), check_vma=False)
```

```python
import functools
import jax
import jax.numpy as jnp
from jax import lax
from jax.experimental import pallas as pl
from jax.experimental.pallas import tpu as pltpu
from jax.sharding import PartitionSpec as P

LIVE = 21841
SMOOTHING = 1.0
TILE = 512
LANES = 128
HALF = LANES // 2
DEEP = 3
NT = (((1,), (1,)), ((), ()))
GROUP = 128
f32, bf16 = jnp.float32, jnp.bfloat16
VMEM = pltpu.VMEM
WHOLE = pl.BlockSpec(memory_space=VMEM)
SCALARS = pl.BlockSpec(memory_space=pltpu.SMEM)
ANYWHERE = pl.BlockSpec(memory_space=pl.ANY)
MIB = 2**20
FREE = pl.CostEstimate(flops=1000, bytes_accessed=1000, transcendentals=0)


def column_tiles(width):
    return [(a, min(a + TILE, width)) for a in range(0, width, TILE)]


def round_up(n, m):
    return -(-n // m) * m


def resident(x):
    return pltpu.with_memory_space_constraint(x, VMEM)


def exchange_plan(peers):
    direct = list(range(2, peers, 2))

    def cut(blocks):
        return [blocks[i : i + 4] for i in range(0, len(blocks), 4)]

    return [2] + direct[1:] + [3, 1], direct[1:], cut(direct + [1]), cut([3] + [b ^ 1 for b in direct[1:]])


def outside(x):
    return pltpu.with_memory_space_constraint(x, pltpu.HBM)


HBM = pl.BlockSpec(memory_space=pltpu.HBM)


def table_kernel(here_ref, requests_hbm, e_hbm, neighbours_hbm, weights_hbm, mine_ref, out_ref, table_ref, near_ref, weight_ref, requests_ref, sems):
    core, me = here_ref[1], here_ref[2]
    rows, depth = e_hbm.shape
    half = rows // 2
    peers, cap = requests_hbm.shape
    k = near_ref.shape[0]
    slots = round_up(k, 8)
    start = pl.multiple_of(core * half, 16)
    moves = (
        (requests_hbm, requests_ref),
        (neighbours_hbm, near_ref),
        (weights_hbm, weight_ref),
        (e_hbm.at[pl.ds(start, half), :], mine_ref.at[:, :depth]),
    )
    copies = [pltpu.make_async_copy(src, dst, sems.at[i]) for i, (src, dst) in enumerate(moves)]
    for copy in copies:
        copy.start()
    table_ref[...] = jnp.zeros_like(table_ref)
    for copy in copies[:3]:
        copy.wait()
    near = near_ref[...]
    slot = near - rows
    block = jnp.zeros_like(near) + me
    within = near
    for p in range(peers):
        block = jnp.where(slot >= p * cap, p, block)
        for j in range(cap):
            within = jnp.where(slot == p * cap + j, requests_ref[p, j], within)
    weight = weight_ref[...]
    w0 = weight.astype(bf16).astype(f32)
    w1 = (weight - w0).astype(bf16).astype(f32)
    w2 = weight - w0 - w1
    for i, x in enumerate((block.astype(f32), within.astype(f32), w0, w1, w2)):
        table_ref[i * slots : i * slots + k, :] = x
    out_ref[...] = table_ref[...].T.astype(bf16)
    mine_ref[:, depth:] = out_ref[pl.ds(start, half), :]
    copies[3].wait()


def tables_of(here, requests, embeddings, neighbours, weights):
    rows, depth = embeddings.shape
    k = neighbours.shape[1]
    return pl.pallas_call(
        table_kernel,
        in_specs=[SCALARS] + [HBM] * 4,
        out_specs=[WHOLE] * 2,
        out_shape=[VMEM((rows // 2, depth + LANES), bf16), VMEM((rows, LANES), bf16)],
        scratch_shapes=[
            VMEM((LANES, rows), f32),
            VMEM((k, rows), jnp.int32),
            VMEM((k, rows), f32),
            pltpu.SMEM(requests.shape, jnp.int32),
            pltpu.SemaphoreType.DMA((4,)),
        ],
        compiler_params=pltpu.CompilerParams(vmem_limit_bytes=MIB),
        cost_estimate=pl.CostEstimate(flops=3 * 10**10, bytes_accessed=10**8, transcendentals=0),
        name="tables",
    )(here, outside(requests), outside(embeddings), outside(neighbours.T), outside(weights.T))


def split(x):
    hi = x.astype(bf16)
    return hi, (x - hi.astype(f32)).astype(bf16)


def dot(a, b):
    return jnp.dot(a, b, preferred_element_type=f32)


def add_powers(tiles, min_live, here_ref, e_ref, ct_ref, p_ref, rows, stat_ref, before=None):
    n = e_ref.shape[0]
    lane = lax.broadcasted_iota(jnp.int32, (n, LANES), 1)
    stat = jnp.where(lane < HALF, -1e30, 0.0)
    for t, (a, b) in enumerate(tiles):
        if before:
            before(t)
        logits = lax.dot_general(e_ref[...], ct_ref[a:b, :], NT, preferred_element_type=f32)
        if b > min_live:
            live = lax.broadcasted_iota(jnp.int32, logits.shape, 1) + a < here_ref[0]
            logits = jnp.where(live, logits, -1e30)
        top = jnp.max(logits, axis=1, keepdims=True)
        powers = jnp.exp(logits - top)
        if b > min_live:
            powers = jnp.where(live, powers, 0.0)
        p_ref[rows, a:b] = powers
        stat = jnp.where(lane == t, top, stat)
        stat = jnp.where(lane == t + HALF, jnp.sum(powers, axis=1, keepdims=True), stat)
    stat_ref[rows, :] = stat
    return stat


def row_stats(stat, slots):
    turned = stat.T
    tops, sums = turned[:slots], turned[HALF : HALF + slots]
    top = jnp.max(tops, axis=0, keepdims=True)
    return tops, jnp.concatenate([top, jnp.sum(sums * jnp.exp(tops - top), axis=0, keepdims=True)], axis=0)


def powers_kernel(tiles, min_live, depth, first_row, n_parts, final, here_ref, *refs):
    parts, ct_ref = refs[:n_parts], refs[n_parts]
    p_ref, tab_ref, stat_ref, *ends, e_ref = refs[n_parts + (6 if final else 4) :]
    if final:
        tile_ref, both_ref = ends
        slots = tile_ref.shape[0]
        tops, both = refs[n_parts + 4][...], refs[n_parts + 5][...]
    core = here_ref[1]
    row = 0
    for i, part in enumerate(parts):
        n = part.shape[0]
        at = pl.multiple_of(row + n * (-core if i % 2 else core), 16)
        e_ref[pl.ds(at, n), :] = part[:, :depth]
        tab_ref[pl.ds(first_row + at, n), :] = part[:, depth:].astype(f32)
        row += n
    stat = add_powers(tiles, min_live, here_ref, e_ref, ct_ref, p_ref, slice(first_row, first_row + row), stat_ref)
    if final:
        own_tops, own_both = row_stats(stat, slots)
        tile_ref[...] = jnp.concatenate([tops, own_tops], axis=1)
        both_ref[...] = jnp.concatenate([both, own_both], axis=1)


def powers_shapes(total_rows, width):
    return [VMEM((total_rows, width), f32), VMEM((total_rows, LANES), f32), VMEM((total_rows, LANES), f32)]


def powers_of(parts, ct, here, buffers, first_row, min_live, earlier=()):
    width, depth = ct.shape
    rows = sum(p.shape[0] for p in parts)
    total_rows = buffers[0].shape[0]
    tiles = column_tiles(width)
    final = bool(earlier)
    n = len(parts)
    shapes = powers_shapes(total_rows, width)
    if final:
        shapes += [VMEM((round_up(len(tiles), 8), total_rows), f32), VMEM((2, total_rows), f32)]
    return pl.pallas_call(
        functools.partial(powers_kernel, tiles, min_live, depth, first_row, n, final),
        in_specs=[SCALARS] + [WHOLE] * (n + 4 + len(earlier)),
        out_specs=[WHOLE] * len(shapes),
        out_shape=shapes,
        scratch_shapes=[VMEM((rows, depth), bf16)],
        input_output_aliases={2 + n + i: i for i in range(3)},
        compiler_params=pltpu.CompilerParams(vmem_limit_bytes=8 * MIB),
        cost_estimate=FREE,
        name="powers",
    )(here, *[resident(x) for x in parts], ct, *[resident(x) for x in (*buffers, *earlier)])


def early_kernel(rows, stat_ref, tile_ref, both_ref):
    tile_ref[...], both_ref[...] = row_stats(stat_ref[:rows, :], tile_ref.shape[0])


def early_stats(stat, rows, n_tiles):
    return pl.pallas_call(
        functools.partial(early_kernel, rows),
        in_specs=[WHOLE],
        out_specs=[WHOLE] * 2,
        out_shape=[VMEM((round_up(n_tiles, 8), rows), f32), VMEM((2, rows), f32)],
        compiler_params=pltpu.CompilerParams(vmem_limit_bytes=4 * MIB),
        cost_estimate=FREE,
        name="early",
    )(resident(stat))


def place_of(order, rows_here, me, block, within):
    relative = block ^ me
    place = jnp.zeros_like(block)
    for i, b in enumerate(order):
        place = jnp.where(relative == b, i * rows_here, place)
    return place + within


def second_rows(order, rows_here, me, k, tab, itself, total_rows):
    n, slots = tab.shape[0], round_up(k, 8)
    within = pltpu.roll(tab, LANES - slots, 1).astype(jnp.int32)
    weight = pltpu.roll(tab, LANES - 2 * slots, 1) + pltpu.roll(tab, LANES - 3 * slots, 1) + pltpu.roll(tab, LANES - 4 * slots, 1)
    place = place_of(order, rows_here, me, tab.astype(jnp.int32), within)
    column = lax.broadcasted_iota(jnp.int32, (n, total_rows), 1)
    acc = jnp.where(column == itself, 1.0, 0.0)
    degree = jnp.zeros((n, 1), f32)
    for i in range(k):
        w = weight[:, i : i + 1]
        acc = acc + jnp.where(column == place[:, i : i + 1], SMOOTHING * w, 0.0)
        degree = degree + w
    return split(acc * (1.0 / (1.0 + SMOOTHING * degree)))


def own_kernel(tiles, min_live, order, here_ref, table_ref, own_ref, ct_ref, requests_hbm, near_hbm, weight_hbm, *refs):
    p_ref, tab_ref, stat_ref, m_ref, whi_ref, wlo_ref, asked_ref, pick_ref = refs[:8]
    row_ref, near_ref, weight_ref, requests_ref, sems = refs[8:]
    me = here_ref[2]
    peers, cap = requests_hbm.shape
    k, rows_here = near_hbm.shape
    total_rows = tab_ref.shape[0]
    moves = (
        (requests_hbm, requests_ref),
        (near_hbm, near_ref),
        (weight_hbm, weight_ref),
    )
    copies = [pltpu.make_async_copy(src, dst, sems.at[i]) for i, (src, dst) in enumerate(moves)]
    for copy in copies:
        copy.start()
    tab = table_ref[...].astype(f32)
    tab_ref[:rows_here, :] = tab
    row_ref[...] = jnp.full_like(row_ref, -1)
    for copy in copies:
        copy.wait()

    lane = lax.broadcasted_iota(jnp.int32, (1, LANES), 1)
    for p in range(peers):
        start = place_of(order, rows_here, me, jnp.full((1, 1), p, jnp.int32), 0)
        row = jnp.full((1, LANES), -1, jnp.int32)
        for j in range(cap):
            row = jnp.where(lane == j, requests_ref[p, j], row)
        row_ref[p : p + 1, :] = jnp.where(row >= 0, row + start, -1)
    asked = row_ref[...].T
    column = lax.broadcasted_iota(jnp.int32, (cap, total_rows), 1)
    for p in range(peers):
        one = asked[:cap, p : p + 1]
        asked_ref[p * cap : (p + 1) * cap, :] = jnp.broadcast_to(one, (cap, LANES))
        pick_ref[p * cap : (p + 1) * cap, :] = jnp.where(column == one, 1.0, 0.0).astype(bf16)

    near, weight = near_ref[...].T, weight_ref[...].T
    scale = 1.0 / (1.0 + SMOOTHING * jnp.sum(weight, axis=1, keepdims=True))

    def edges(offset, n):
        column = lax.broadcasted_iota(jnp.int32, (rows_here, n), 1) + offset
        acc = jnp.zeros((rows_here, n), f32)
        for i in range(k):
            acc = acc + jnp.where(column == near[:, i : i + 1], SMOOTHING * weight[:, i : i + 1], 0.0)
        return split(acc * scale)

    whi_ref[...], wlo_ref[...] = edges(rows_here, whi_ref.shape[1])
    whi, wlo = edges(0, rows_here)
    itself = lax.broadcasted_iota(jnp.int32, (rows_here, 1), 0)
    thi, tlo = second_rows(order, rows_here, me, k, tab, itself, total_rows)
    own = jnp.where(lax.broadcasted_iota(jnp.int32, (rows_here, total_rows), 1) == itself, scale, 0.0)
    m_ref[...] = own + dot(whi, thi) + dot(wlo, thi) + dot(whi, tlo)
    add_powers(tiles, min_live, here_ref, own_ref, ct_ref, p_ref, slice(0, rows_here), stat_ref)


def own_powers(here, table, embeddings, requests, neighbours, weights, classes, order, total_rows, min_live):
    rows_here, k = neighbours.shape
    width = classes.shape[0]
    tiles = column_tiles(width)
    shapes = powers_shapes(total_rows, width) + [
        VMEM((rows_here, total_rows), f32),
        VMEM((rows_here, requests.size), bf16),
        VMEM((rows_here, requests.size), bf16),
        VMEM((requests.size, LANES), jnp.int32),
        VMEM((requests.size, total_rows), bf16),
    ]
    return pl.pallas_call(
        functools.partial(own_kernel, tiles, min_live, order),
        in_specs=[SCALARS] + [WHOLE] * 3 + [HBM] * 3,
        out_specs=[WHOLE] * len(shapes),
        out_shape=shapes,
        scratch_shapes=[
            VMEM((LANES, LANES), jnp.int32),
            VMEM((k, rows_here), jnp.int32),
            VMEM((k, rows_here), f32),
            pltpu.SMEM(requests.shape, jnp.int32),
            pltpu.SemaphoreType.DMA((3,)),
        ],
        compiler_params=pltpu.CompilerParams(vmem_limit_bytes=(8 if total_rows <= 768 else 14) * MIB),
        cost_estimate=FREE,
        name="own",
    )(here, resident(table), embeddings, classes, *[outside(x) for x in (requests, neighbours.T, weights.T)])


def graph_kernel(order, k, here_ref, m_ref, whi_ref, wlo_ref, asked_ref, pick_ref, tab_ref, out_ref):
    rows_here, total_rows = m_ref.shape
    asked = whi_ref.shape[1]
    tab = dot(pick_ref[...], tab_ref[...].astype(bf16))
    acc = m_ref[...]
    for start in range(0, asked, GROUP):
        rows = slice(start, min(start + GROUP, asked))
        thi, tlo = second_rows(order, rows_here, here_ref[2], k, tab[rows], asked_ref[rows, :1], total_rows)
        whi, wlo = whi_ref[:, rows], wlo_ref[:, rows]
        acc = acc + dot(whi, thi) + dot(wlo, thi) + dot(whi, tlo)
    out_ref[...] = acc


def graph_of(here, edges, tab, order, k):
    total_rows = tab.shape[0]
    return pl.pallas_call(
        functools.partial(graph_kernel, order, k),
        in_specs=[SCALARS] + [WHOLE] * 6,
        out_specs=WHOLE,
        out_shape=VMEM(edges[0].shape, f32),
        compiler_params=pltpu.CompilerParams(vmem_limit_bytes=(6 if total_rows <= 768 else 20) * MIB),
        cost_estimate=FREE,
        name="graph",
    )(here, *[resident(x) for x in edges], resident(tab))


def apply_kernel(tiles, m_ref, p_ref, tile_ref, *refs):
    *stat_refs, out_ref, _, staged, sems = refs
    rows_here = m_ref.shape[0]
    tops = [r[i : i + 1, :] for r in stat_refs for i in (0, 2)]
    sums = [r[i : i + 1, :] for r in stat_refs for i in (1, 3)]
    top = functools.reduce(jnp.maximum, tops)
    total = sum(s * jnp.exp(t - top) for s, t in zip(sums, tops))
    factors = jnp.exp(tile_ref[...] - top) / total
    copies = []
    for t, (a, b) in enumerate(tiles):
        whi, wlo = split(m_ref[...] * factors[t : t + 1, :])
        hi, lo = split(p_ref[:, a:b])
        x = dot(jnp.concatenate([whi, wlo], axis=0), hi)
        staged[:, a:b] = x[:rows_here] + x[rows_here:] + dot(whi, lo)
        copy = pltpu.make_async_copy(staged.at[:, a:b], out_ref.at[:, a:b], sems.at[t])
        copy.start()
        copies.append(copy)
    for copy in copies:
        copy.wait()


def applied(m, powers, tile_tops, stats):
    rows_here, width = m.shape[0], powers.shape[1]
    total_rows = m.shape[1]
    tiles = column_tiles(width)
    operands = [m, powers, tile_tops, *stats]
    return pl.pallas_call(
        functools.partial(apply_kernel, tiles),
        in_specs=[WHOLE] * len(operands),
        out_specs=[ANYWHERE, WHOLE],
        out_shape=[jax.ShapeDtypeStruct((rows_here, width), f32), VMEM(powers.shape, f32)],
        input_output_aliases={1: 1},
        scratch_shapes=[VMEM((rows_here, width), f32), pltpu.SemaphoreType.DMA((len(tiles),))],
        compiler_params=pltpu.CompilerParams(vmem_limit_bytes=(8 if total_rows <= 768 else 16) * MIB),
        cost_estimate=FREE,
        name="smooth",
    )(*[resident(x) for x in operands])[0]


def shards(n_img, n_cls, embeddings, class_text_embedding, neighbours, weights, requests):
    rows_here = embeddings.shape[0]
    width = class_text_embedding.shape[1]
    half = rows_here // 2
    me, col = lax.axis_index("img"), lax.axis_index("cls")
    total_rows = n_img * rows_here
    here = jnp.stack([jnp.minimum(LIVE - col * width, width), col & 1, me]).astype(jnp.int32)
    min_live = min(width, LIVE - (n_cls - 1) * width)

    classes = class_text_embedding.T
    mine, table = tables_of(here, requests[0], embeddings, neighbours, weights)
    first, relayed, beside, last = exchange_plan(n_img)
    order = [0] + [b for piece in beside + last for b in piece]

    def swap(x):
        return lax.ppermute(x, "cls", [(i, i ^ 1) for i in range(n_cls)])

    def exchange(x, step):
        return lax.ppermute(x, "img", [(i, i ^ step) for i in range(n_img)])

    def halves(x, blocks):
        other = swap(x)
        cuts = [slice(i * half, (i + 1) * half) for i in range(len(blocks))]
        return {b: [x[c], other[c]] for b, c in zip(blocks, cuts)}

    held = [exchange(mine, b) for b in first]
    results = own_powers(here, table, embeddings, requests[0], neighbours, weights, classes, order, total_rows, min_live)
    buffers, first_row, edges = list(results[:3]), rows_here, results[3:]

    def work(blocks, earlier=()):
        nonlocal buffers, first_row
        parts = [x for b in blocks for x in pairs[b]]
        buffers = list(powers_of(parts, classes, here, buffers, first_row, min_live, earlier))
        first_row += len(blocks) * rows_here

    *held, buffers[2] = lax.optimization_barrier((*held, buffers[2]))
    got = exchange(jnp.concatenate([x for b, x in zip(first, held) if b in relayed], axis=0), 1)
    pairs = halves(jnp.concatenate(held, axis=0), first)
    for piece in beside:
        work(piece)
    got, buffers[2] = lax.optimization_barrier((got, buffers[2]))
    pairs |= halves(got, [b ^ 1 for b in relayed])
    for piece in last[:-1]:
        work(piece)
    work(last[-1], early_stats(buffers[2], first_row, len(column_tiles(width))))
    powers, tab, _, tile_tops, stats = buffers
    stats = jnp.concatenate([stats, swap(stats)], axis=0)
    stats, tab = lax.optimization_barrier((stats, tab))
    far = [lax.ppermute(stats, "cls", [(i, i ^ d) for i in range(n_cls)]) for d in range(2, n_cls, 2)]
    m = graph_of(here, edges, tab, order, neighbours.shape[1])
    return applied(m, powers, tile_tops, [stats, *far])


def solution(mesh):
    in_specs = (
        P("img", None),
        P(None, "cls"),
        P("img", None),
        P("img", None),
        P("img", None, None),
    )
    sizes = mesh.shape
    run = functools.partial(shards, sizes["img"], sizes["cls"])
    return jax.shard_map(run, mesh=mesh, in_specs=in_specs, out_specs=P("img", "cls"), check_vma=False)
```

```python
import functools
import jax
import jax.numpy as jnp
from jax import lax
from jax.experimental import pallas as pl
from jax.experimental.pallas import tpu as pltpu
from jax.sharding import PartitionSpec as P

LIVE = 21841
SMOOTHING = 1.0
TILE = 512
LANES = 128
HALF = LANES // 2
DEEP = 3
NT = (((1,), (1,)), ((), ()))
GROUP = 128
f32, bf16 = jnp.float32, jnp.bfloat16
VMEM = pltpu.VMEM
WHOLE = pl.BlockSpec(memory_space=VMEM)
SCALARS = pl.BlockSpec(memory_space=pltpu.SMEM)
ANYWHERE = pl.BlockSpec(memory_space=pl.ANY)
MIB = 2**20
FREE = pl.CostEstimate(flops=1000, bytes_accessed=1000, transcendentals=0)


def column_tiles(width):
    return [(a, min(a + TILE, width)) for a in range(0, width, TILE)]


def round_up(n, m):
    return -(-n // m) * m


def resident(x):
    return pltpu.with_memory_space_constraint(x, VMEM)


def exchange_plan(peers):
    direct = list(range(2, peers, 2))

    def cut(blocks):
        return [blocks[i : i + 4] for i in range(0, len(blocks), 4)]

    return [2] + direct[1:] + [3, 1], direct[1:], cut(direct + [1]), cut([3] + [b ^ 1 for b in direct[1:]])


def outside(x):
    return pltpu.with_memory_space_constraint(x, pltpu.HBM)


HBM = pl.BlockSpec(memory_space=pltpu.HBM)


def table_kernel(here_ref, requests_hbm, e_hbm, neighbours_hbm, weights_hbm, mine_ref, out_ref, table_ref, near_ref, weight_ref, requests_ref, sems):
    core, me = here_ref[1], here_ref[2]
    rows, depth = e_hbm.shape
    half = rows // 2
    peers, cap = requests_hbm.shape
    k = near_ref.shape[0]
    slots = round_up(k, 8)
    start = pl.multiple_of(core * half, 16)
    moves = (
        (requests_hbm, requests_ref),
        (neighbours_hbm, near_ref),
        (weights_hbm, weight_ref),
        (e_hbm.at[pl.ds(start, half), :], mine_ref.at[:, :depth]),
    )
    copies = [pltpu.make_async_copy(src, dst, sems.at[i]) for i, (src, dst) in enumerate(moves)]
    for copy in copies:
        copy.start()
    table_ref[...] = jnp.zeros_like(table_ref)
    for copy in copies[:3]:
        copy.wait()
    near = near_ref[...]
    slot = near - rows
    block = jnp.zeros_like(near) + me
    within = near
    for p in range(peers):
        block = jnp.where(slot >= p * cap, p, block)
        for j in range(cap):
            within = jnp.where(slot == p * cap + j, requests_ref[p, j], within)
    weight = weight_ref[...]
    w0 = weight.astype(bf16).astype(f32)
    w1 = (weight - w0).astype(bf16).astype(f32)
    w2 = weight - w0 - w1
    for i, x in enumerate((block.astype(f32), within.astype(f32), w0, w1, w2)):
        table_ref[i * slots : i * slots + k, :] = x
    out_ref[...] = table_ref[...].T.astype(bf16)
    mine_ref[:, depth:] = out_ref[pl.ds(start, half), :]
    copies[3].wait()


def tables_of(here, requests, embeddings, neighbours, weights):
    rows, depth = embeddings.shape
    k = neighbours.shape[1]
    return pl.pallas_call(
        table_kernel,
        in_specs=[SCALARS] + [HBM] * 4,
        out_specs=[WHOLE] * 2,
        out_shape=[VMEM((rows // 2, depth + LANES), bf16), VMEM((rows, LANES), bf16)],
        scratch_shapes=[
            VMEM((LANES, rows), f32),
            VMEM((k, rows), jnp.int32),
            VMEM((k, rows), f32),
            pltpu.SMEM(requests.shape, jnp.int32),
            pltpu.SemaphoreType.DMA((4,)),
        ],
        compiler_params=pltpu.CompilerParams(vmem_limit_bytes=MIB),
        cost_estimate=pl.CostEstimate(flops=3 * 10**10, bytes_accessed=10**8, transcendentals=0),
        name="tables",
    )(here, outside(requests), outside(embeddings), outside(neighbours.T), outside(weights.T))


def split(x):
    hi = x.astype(bf16)
    return hi, (x - hi.astype(f32)).astype(bf16)


def dot(a, b):
    return jnp.dot(a, b, preferred_element_type=f32)


def add_powers(tiles, min_live, here_ref, e_ref, ct_ref, p_ref, rows, stat_ref, before=None):
    n = e_ref.shape[0]
    lane = lax.broadcasted_iota(jnp.int32, (n, LANES), 1)
    stat = jnp.where(lane < HALF, -1e30, 0.0)
    for t, (a, b) in enumerate(tiles):
        if before:
            before(t)
        logits = lax.dot_general(e_ref[...], ct_ref[a:b, :], NT, preferred_element_type=f32)
        if b > min_live:
            live = lax.broadcasted_iota(jnp.int32, logits.shape, 1) + a < here_ref[0]
            logits = jnp.where(live, logits, -1e30)
        top = jnp.max(logits, axis=1, keepdims=True)
        powers = jnp.exp(logits - top)
        if b > min_live:
            powers = jnp.where(live, powers, 0.0)
        p_ref[rows, a:b] = powers
        stat = jnp.where(lane == t, top, stat)
        stat = jnp.where(lane == t + HALF, jnp.sum(powers, axis=1, keepdims=True), stat)
    stat_ref[rows, :] = stat
    return stat


def row_stats(stat, slots):
    turned = stat.T
    tops, sums = turned[:slots], turned[HALF : HALF + slots]
    top = jnp.max(tops, axis=0, keepdims=True)
    return tops, jnp.concatenate([top, jnp.sum(sums * jnp.exp(tops - top), axis=0, keepdims=True)], axis=0)


def powers_kernel(tiles, min_live, depth, first_row, n_parts, final, here_ref, *refs):
    parts, ct_ref = refs[:n_parts], refs[n_parts]
    p_ref, tab_ref, stat_ref, *ends, e_ref = refs[n_parts + 4 :]
    if final:
        tile_ref, both_ref = ends
        slots = tile_ref.shape[0]
        tops, both = row_stats(stat_ref[:first_row, :], slots)
    core = here_ref[1]
    row = 0
    for i, part in enumerate(parts):
        n = part.shape[0]
        at = pl.multiple_of(row + n * (-core if i % 2 else core), 16)
        e_ref[pl.ds(at, n), :] = part[:, :depth]
        tab_ref[pl.ds(first_row + at, n), :] = part[:, depth:].astype(f32)
        row += n
    stat = add_powers(tiles, min_live, here_ref, e_ref, ct_ref, p_ref, slice(first_row, first_row + row), stat_ref)
    if final:
        own_tops, own_both = row_stats(stat, slots)
        tile_ref[...] = jnp.concatenate([tops, own_tops], axis=1)
        both_ref[...] = jnp.concatenate([both, own_both], axis=1)


def powers_shapes(total_rows, width):
    return [VMEM((total_rows, width), f32), VMEM((total_rows, LANES), f32), VMEM((total_rows, LANES), f32)]


def powers_of(parts, ct, here, buffers, first_row, min_live):
    width, depth = ct.shape
    rows = sum(p.shape[0] for p in parts)
    total_rows = buffers[0].shape[0]
    tiles = column_tiles(width)
    final = first_row + rows == total_rows
    n = len(parts)
    shapes = powers_shapes(total_rows, width)
    if final:
        shapes += [VMEM((round_up(len(tiles), 8), total_rows), f32), VMEM((2, total_rows), f32)]
    return pl.pallas_call(
        functools.partial(powers_kernel, tiles, min_live, depth, first_row, n, final),
        in_specs=[SCALARS] + [WHOLE] * (n + 4),
        out_specs=[WHOLE] * len(shapes),
        out_shape=shapes,
        scratch_shapes=[VMEM((rows, depth), bf16)],
        input_output_aliases={2 + n + i: i for i in range(3)},
        compiler_params=pltpu.CompilerParams(vmem_limit_bytes=8 * MIB),
        cost_estimate=FREE,
        name="powers",
    )(here, *[resident(x) for x in parts], ct, *[resident(x) for x in buffers])


def place_of(order, rows_here, me, block, within):
    relative = block ^ me
    place = jnp.zeros_like(block)
    for i, b in enumerate(order):
        place = jnp.where(relative == b, i * rows_here, place)
    return place + within


def second_rows(order, rows_here, me, k, tab, itself, total_rows):
    n, slots = tab.shape[0], round_up(k, 8)
    within = pltpu.roll(tab, LANES - slots, 1).astype(jnp.int32)
    weight = pltpu.roll(tab, LANES - 2 * slots, 1) + pltpu.roll(tab, LANES - 3 * slots, 1) + pltpu.roll(tab, LANES - 4 * slots, 1)
    place = place_of(order, rows_here, me, tab.astype(jnp.int32), within)
    column = lax.broadcasted_iota(jnp.int32, (n, total_rows), 1)
    acc = jnp.where(column == itself, 1.0, 0.0)
    degree = jnp.zeros((n, 1), f32)
    for i in range(k):
        w = weight[:, i : i + 1]
        acc = acc + jnp.where(column == place[:, i : i + 1], SMOOTHING * w, 0.0)
        degree = degree + w
    return split(acc * (1.0 / (1.0 + SMOOTHING * degree)))


def own_kernel(tiles, min_live, order, here_ref, requests_ref, table_ref, own_ref, ct_ref, near_ref, weight_ref, *refs):
    p_ref, tab_ref, stat_ref, m_ref, whi_ref, wlo_ref, asked_ref, pick_ref = refs[:8]
    row_ref = refs[8]
    me = here_ref[2]
    peers, cap = requests_ref.shape
    k, rows_here = near_ref.shape
    total_rows = tab_ref.shape[0]
    tab = table_ref[...].astype(f32)
    tab_ref[:rows_here, :] = tab
    row_ref[...] = jnp.full_like(row_ref, -1)

    lane = lax.broadcasted_iota(jnp.int32, (1, LANES), 1)
    for p in range(peers):
        start = place_of(order, rows_here, me, jnp.full((1, 1), p, jnp.int32), 0)
        row = jnp.full((1, LANES), -1, jnp.int32)
        for j in range(cap):
            row = jnp.where(lane == j, requests_ref[p, j], row)
        row_ref[p : p + 1, :] = jnp.where(row >= 0, row + start, -1)
    asked = row_ref[...].T
    column = lax.broadcasted_iota(jnp.int32, (cap, total_rows), 1)
    for p in range(peers):
        one = asked[:cap, p : p + 1]
        asked_ref[p * cap : (p + 1) * cap, :] = jnp.broadcast_to(one, (cap, LANES))
        pick_ref[p * cap : (p + 1) * cap, :] = jnp.where(column == one, 1.0, 0.0).astype(bf16)

    near, weight = near_ref[...].T, weight_ref[...].T
    scale = 1.0 / (1.0 + SMOOTHING * jnp.sum(weight, axis=1, keepdims=True))

    def edges(offset, n):
        column = lax.broadcasted_iota(jnp.int32, (rows_here, n), 1) + offset
        acc = jnp.zeros((rows_here, n), f32)
        for i in range(k):
            acc = acc + jnp.where(column == near[:, i : i + 1], SMOOTHING * weight[:, i : i + 1], 0.0)
        return split(acc * scale)

    whi_ref[...], wlo_ref[...] = edges(rows_here, whi_ref.shape[1])
    whi, wlo = edges(0, rows_here)
    itself = lax.broadcasted_iota(jnp.int32, (rows_here, 1), 0)
    thi, tlo = second_rows(order, rows_here, me, k, tab, itself, total_rows)
    own = jnp.where(lax.broadcasted_iota(jnp.int32, (rows_here, total_rows), 1) == itself, scale, 0.0)
    m_ref[...] = own + dot(whi, thi) + dot(wlo, thi) + dot(whi, tlo)
    add_powers(tiles, min_live, here_ref, own_ref, ct_ref, p_ref, slice(0, rows_here), stat_ref)


def own_powers(here, table, embeddings, requests, neighbours, weights, classes, order, total_rows, min_live):
    rows_here, k = neighbours.shape
    width = classes.shape[0]
    tiles = column_tiles(width)
    shapes = powers_shapes(total_rows, width) + [
        VMEM((rows_here, total_rows), f32),
        VMEM((rows_here, requests.size), bf16),
        VMEM((rows_here, requests.size), bf16),
        VMEM((requests.size, LANES), jnp.int32),
        VMEM((requests.size, total_rows), bf16),
    ]
    return pl.pallas_call(
        functools.partial(own_kernel, tiles, min_live, order),
        in_specs=[SCALARS, SCALARS] + [WHOLE] * 5,
        out_specs=[WHOLE] * len(shapes),
        out_shape=shapes,
        scratch_shapes=[
            VMEM((LANES, LANES), jnp.int32),
        ],
        compiler_params=pltpu.CompilerParams(vmem_limit_bytes=(8 if total_rows <= 768 else 14) * MIB),
        cost_estimate=FREE,
        name="own",
    )(here, requests, resident(table), embeddings, classes, neighbours.T, weights.T)


def graph_kernel(order, k, here_ref, m_ref, whi_ref, wlo_ref, asked_ref, pick_ref, tab_ref, out_ref):
    rows_here, total_rows = m_ref.shape
    asked = whi_ref.shape[1]
    tab = dot(pick_ref[...], tab_ref[...].astype(bf16))
    acc = m_ref[...]
    for start in range(0, asked, GROUP):
        rows = slice(start, min(start + GROUP, asked))
        thi, tlo = second_rows(order, rows_here, here_ref[2], k, tab[rows], asked_ref[rows, :1], total_rows)
        whi, wlo = whi_ref[:, rows], wlo_ref[:, rows]
        acc = acc + dot(whi, thi) + dot(wlo, thi) + dot(whi, tlo)
    out_ref[...] = acc


def graph_of(here, edges, tab, order, k):
    total_rows = tab.shape[0]
    return pl.pallas_call(
        functools.partial(graph_kernel, order, k),
        in_specs=[SCALARS] + [WHOLE] * 6,
        out_specs=WHOLE,
        out_shape=VMEM(edges[0].shape, f32),
        compiler_params=pltpu.CompilerParams(vmem_limit_bytes=(6 if total_rows <= 768 else 20) * MIB),
        cost_estimate=FREE,
        name="graph",
    )(here, *[resident(x) for x in edges], resident(tab))


def apply_kernel(tiles, m_ref, p_ref, tile_ref, *refs):
    *stat_refs, out_ref, _, staged, sems = refs
    rows_here = m_ref.shape[0]
    tops = [r[i : i + 1, :] for r in stat_refs for i in (0, 2)]
    sums = [r[i : i + 1, :] for r in stat_refs for i in (1, 3)]
    top = functools.reduce(jnp.maximum, tops)
    total = sum(s * jnp.exp(t - top) for s, t in zip(sums, tops))
    factors = jnp.exp(tile_ref[...] - top) / total
    copies = []
    for t, (a, b) in enumerate(tiles):
        whi, wlo = split(m_ref[...] * factors[t : t + 1, :])
        hi, lo = split(p_ref[:, a:b])
        x = dot(jnp.concatenate([whi, wlo], axis=0), hi)
        staged[:, a:b] = x[:rows_here] + x[rows_here:] + dot(whi, lo)
        copy = pltpu.make_async_copy(staged.at[:, a:b], out_ref.at[:, a:b], sems.at[t])
        copy.start()
        copies.append(copy)
    for copy in copies:
        copy.wait()


def applied(m, powers, tile_tops, stats):
    rows_here, width = m.shape[0], powers.shape[1]
    total_rows = m.shape[1]
    tiles = column_tiles(width)
    operands = [m, powers, tile_tops, *stats]
    return pl.pallas_call(
        functools.partial(apply_kernel, tiles),
        in_specs=[WHOLE] * len(operands),
        out_specs=[ANYWHERE, WHOLE],
        out_shape=[jax.ShapeDtypeStruct((rows_here, width), f32), VMEM(powers.shape, f32)],
        input_output_aliases={1: 1},
        scratch_shapes=[VMEM((rows_here, width), f32), pltpu.SemaphoreType.DMA((len(tiles),))],
        compiler_params=pltpu.CompilerParams(vmem_limit_bytes=(8 if total_rows <= 768 else 16) * MIB),
        cost_estimate=FREE,
        name="smooth",
    )(*[resident(x) for x in operands])[0]


def shards(n_img, n_cls, embeddings, class_text_embedding, neighbours, weights, requests):
    rows_here = embeddings.shape[0]
    width = class_text_embedding.shape[1]
    half = rows_here // 2
    me, col = lax.axis_index("img"), lax.axis_index("cls")
    total_rows = n_img * rows_here
    here = jnp.stack([jnp.minimum(LIVE - col * width, width), col & 1, me]).astype(jnp.int32)
    min_live = min(width, LIVE - (n_cls - 1) * width)

    classes = class_text_embedding.T
    mine, table = tables_of(here, requests[0], embeddings, neighbours, weights)
    first, relayed, beside, last = exchange_plan(n_img)
    order = [0] + [b for piece in beside + last for b in piece]

    def swap(x):
        return lax.ppermute(x, "cls", [(i, i ^ 1) for i in range(n_cls)])

    def exchange(x, step):
        return lax.ppermute(x, "img", [(i, i ^ step) for i in range(n_img)])

    def halves(x, blocks):
        other = swap(x)
        cuts = [slice(i * half, (i + 1) * half) for i in range(len(blocks))]
        return {b: [x[c], other[c]] for b, c in zip(blocks, cuts)}

    held = [exchange(mine, b) for b in first]
    results = own_powers(here, table, embeddings, requests[0], neighbours, weights, classes, order, total_rows, min_live)
    buffers, first_row, edges = list(results[:3]), rows_here, results[3:]

    def work(blocks):
        nonlocal buffers, first_row
        parts = [x for b in blocks for x in pairs[b]]
        buffers = list(powers_of(parts, classes, here, buffers, first_row, min_live))
        first_row += len(blocks) * rows_here

    *held, buffers[2] = lax.optimization_barrier((*held, buffers[2]))
    got = exchange(jnp.concatenate([x for b, x in zip(first, held) if b in relayed], axis=0), 1)
    pairs = halves(jnp.concatenate(held, axis=0), first)
    for piece in beside:
        work(piece)
    got, buffers[2] = lax.optimization_barrier((got, buffers[2]))
    pairs |= halves(got, [b ^ 1 for b in relayed])
    for piece in last:
        work(piece)
    powers, tab, _, tile_tops, stats = buffers
    stats = jnp.concatenate([stats, swap(stats)], axis=0)
    stats, tab = lax.optimization_barrier((stats, tab))
    far = [lax.ppermute(stats, "cls", [(i, i ^ d) for i in range(n_cls)]) for d in range(2, n_cls, 2)]
    m = graph_of(here, edges, tab, order, neighbours.shape[1])
    return applied(m, powers, tile_tops, [stats, *far])


def solution(mesh):
    in_specs = (
        P("img", None),
        P(None, "cls"),
        P("img", None),
        P("img", None),
        P("img", None, None),
    )
    sizes = mesh.shape
    run = functools.partial(shards, sizes["img"], sizes["cls"])
    return jax.shard_map(run, mesh=mesh, in_specs=in_specs, out_specs=P("img", "cls"), check_vma=False)
```
